512 devices in a mesh: grp: 16 (over y, z_lo), col: 32 (over x, z_hi, core).
Axes of the slice: x: 4, y: 8, z: 8 (z_hi: 4, z_lo: 2; z = z_hi * 2 + z_lo), core: 2. Of those that a mesh axis runs over, the one named last changes fastest.
Arguments:
- factors: bfloat16 [2048, 16, 1024], P('col', 'grp'), may hold values from -2 to 2
- occ_levels: float32 [16], replicated, may hold values from -2 to -0.3
- vir_levels: float32 [1024], replicated, may hold values from 0.1 to 15
- slot_orbital: int32 [16], replicated, may hold values from 0 to 15, each once
Outputs:
- amplitudes: bfloat16 [16, 1024, 16384], P(None, 'col', 'grp')
- pair_energy: float32 [16, 16], replicated
The draws below stay inside these ranges and needn't reach their ends.
Inputs may be any that keep to these rules, and one draw needn't show every extreme that they name: `slot_orbital`: each slot holds a different orbital.
All inputs are finite; a program needn't handle non-finite values.
Results may differ from the reference program's by a relative error of at most 0.001.
Values may be sent and summed in bfloat16 or wider, within the bound.
No kernel may reach another device: no remote copies, remote signals or barrier semaphores. Data moves between devices by JAX's collectives and lax.ppermute only.
A program may use at most 64 MiB of HBM per device.

```python
import jax
import jax.numpy as jnp
from jax import lax

AUX = 2048
NV = 1024
NOCC = 16


def draw_vir_levels(key, part):
    key = jax.random.fold_in(key, 7)
    position = jnp.arange(NV, dtype=jnp.float32) / NV
    trend = 0.2 * jnp.exp(jnp.log(50.0) * position)
    jitter = jnp.exp(jax.random.uniform(key, (NV,), jnp.float32, -0.35, 0.35))
    return trend * jitter


def spiked(result, own_key, source, target, parts, factor):
    def block_of(dim):
        return (jnp.arange(result.shape[dim]) // (result.shape[dim] // parts)).reshape((-1,) + (1,) * (result.ndim - 1 - dim))

    near = jax.random.permutation(own_key, parts)[block_of(target)]
    other_side = (block_of(target) + parts // 2) % parts
    return jnp.where((block_of(source) == near) | (block_of(source) == other_side), factor * result, result)


def level_of(key, shape, cuts, least, largest):
    loudness, own = 1.0, jax.random.fold_in(key, 6)
    for dim, blocks in cuts:
        draws = jnp.exp(jax.random.uniform(jax.random.fold_in(own, dim), (blocks,), jnp.float32, least / len(cuts), largest / len(cuts)))
        loudness = loudness * jnp.repeat(draws, shape[dim] // blocks).reshape([-1 if axis == dim else 1 for axis in range(len(shape))])
    return loudness


def heavy_noise(stream_key, shape, width, reach, cuts, heavy, held_as=jnp.bfloat16):
    values = width * jax.random.normal(stream_key, shape, jnp.float32)
    if cuts:
        values = values * level_of(stream_key, shape, cuts, -0.22, 0.18)
    return jnp.clip(spiked(values, jax.random.fold_in(stream_key, 3), *heavy), -reach, reach).astype(held_as)


def setup_inputs(seed: int = 0) -> dict:
    keys = jax.random.split(jax.random.key(seed), 5)
    return {
        "factors": heavy_noise(keys[0], (AUX, NOCC, NV), (AUX // 64) ** -0.5, 2.0, ((0, 32), (1, 16)), (0, 2, 32, 2.75)),
        "occ_levels": jnp.clip(jax.random.uniform(keys[1], (NOCC,), jnp.float32, -2.0, -0.3), -2.0, -0.3),
        "vir_levels": draw_vir_levels(jax.random.fold_in(keys[4], 71), 0),
        "slot_orbital": jax.random.permutation(keys[3], NOCC).astype(jnp.int32),
    }


def reference(factors, occ_levels, vir_levels, slot_orbital):
    occ_energy = occ_levels[slot_orbital]
    wide = factors.astype(jnp.float32)

    def per_orbital(orbital):
        first_rows = lax.dynamic_index_in_dim(wide, orbital, 1, keepdims=False)
        integrals = jnp.einsum("pa,pjb->ajb", first_rows, wide)
        occ_pair = lax.dynamic_index_in_dim(occ_energy, orbital, 0, keepdims=False) + occ_energy
        denominator = occ_pair[None, :, None] - vir_levels[:, None, None] - vir_levels[None, None, :]
        amp_block = (integrals / denominator).astype(jnp.bfloat16)
        amp_block = jnp.transpose(amp_block, (0, 2, 1)).reshape(NV, NV * NOCC)
        swapped = jnp.transpose(integrals, (2, 1, 0))
        energy_row = jnp.sum(integrals * (2.0 * integrals - swapped) / denominator, axis=(0, 2))
        return amp_block, energy_row

    amplitudes, energies = lax.map(per_orbital, jnp.arange(NOCC, dtype=jnp.int32))
    return amplitudes, energies / (NV * NV)
```

```python
import functools

import jax
import jax.numpy as jnp
import numpy as np
from jax import lax
from jax.experimental import pallas as pl
from jax.experimental.pallas import tpu as pltpu
from jax.sharding import Mesh, PartitionSpec as P

Y, ZL, X, ZH, K = 8, 2, 4, 4, 2
GRP, COL = Y * ZL, X * ZH * K
AUX, NV, NOCC = 2048, 1024, 16
PB = AUX // COL
WA = NV // COL
WB = NV // GRP
ROWS, COLS = NOCC * WA, NOCC * WB
VMEM = pl.BlockSpec(memory_space=pltpu.VMEM)
SMEM = pl.BlockSpec(memory_space=pltpu.SMEM)
PARAMS = pltpu.CompilerParams(vmem_limit_bytes=48 * 1024 * 1024)


def low_half(rows):
    return lax.broadcasted_iota(jnp.int32, (rows, 128), 1) < 64


def turn(v):
    return pltpu.roll(v.astype(jnp.float32), 64, 1).astype(v.dtype)


def pair_halves(first, second):
    low = low_half(first.shape[0])
    return jnp.where(low, first, turn(second)), jnp.where(low, turn(first), second)


def prep_kernel(x_ref, a1_ref, a2_ref):
    low = low_half(WA // 2)
    for t in range(NV // 128):
        tile = x_ref[:, t * 128 : (t + 1) * 128]
        wide = tile.astype(jnp.float32)
        both = jnp.concatenate([wide, wide], axis=0).T
        for s in range(128 // WA):
            top = both[s * WA : s * WA + WA // 2]
            bottom = both[s * WA + WA // 2 : (s + 1) * WA]
            piece = jnp.where(low, top, bottom).astype(jnp.bfloat16)
            c = t * (128 // WA) + s
            for z in range(ZL):
                a1_ref[z * COL + c] = piece
        even, odd = pair_halves(tile[: PB // 2], tile[PB // 2 :])
        for z in range(ZH):
            a2_ref[(2 * t) * ZH + z] = even
            a2_ref[(2 * t + 1) * ZH + z] = odd


def first_kernel(in_ref, out_ref):
    own = lax.axis_index("k")
    for z in range(ZL):
        for rel in range(K):
            k = own if rel == 0 else 1 - own
            for x in range(X):
                for m in range(ZH // 2):
                    base = z * COL + (x * ZH + 2 * m) * K
                    top, bottom = pair_halves(in_ref[base + k], in_ref[base + K + k])
                    lanes = ((rel * X + x) * ZH + 2 * m) * PB
                    out_ref[z, 0 : WA // 2, lanes : lanes + 128] = top
                    out_ref[z, WA // 2 : WA, lanes : lanes + 128] = bottom


def second_kernel(in_ref, out_ref):
    for z in range(ZH):
        for t in range(NOCC // 2):
            top, bottom = pair_halves(in_ref[(2 * t) * ZH + z], in_ref[(2 * t + 1) * ZH + z])
            for copy in range(X):
                out_ref[copy, z, 0 : PB // 2, t * 128 : (t + 1) * 128] = top
                out_ref[copy, z, PB // 2 : PB, t * 128 : (t + 1) * 128] = bottom


def main_kernel(occ_ref, slot_ref, vir_ref, l_ref, r0_ref, r1_ref, perm_ref, amp_ref, energy_ref, x_ref, t_ref, z_ref, col_ref, v_ref):
    column = (lax.axis_index("x") * ZH + lax.axis_index("zh")) * K + lax.axis_index("k")
    group = lax.axis_index("y") * ZL + lax.axis_index("zl")
    half = AUX // 2
    step = 256

    @pl.loop(0, COLS // step)
    def _(n):
        lanes = pl.ds(pl.multiple_of(n * step, step), step)
        x_ref[:, lanes] = jnp.dot(l_ref[:, :half], r0_ref[:, lanes], preferred_element_type=jnp.float32) + jnp.dot(
            l_ref[:, half:], r1_ref[:, lanes], preferred_element_type=jnp.float32
        )

    first_row = vir_ref[pl.ds(column // 4, 1), :]
    v_ref[...] = jnp.broadcast_to(first_row, (128, 128)).T
    col_ref[...] = v_ref[pl.ds(pl.multiple_of((column % 4) * WA, WA), WA), :]
    second_row = vir_ref[pl.ds(group // 2, 1), :]
    low1 = lax.broadcasted_iota(jnp.int32, (1, 128), 1) < 64
    swapped_row = pltpu.roll(jnp.broadcast_to(second_row, (8, 128)), 64, 1)[:1]
    odd = group % 2 == 1
    v_second = jnp.where(low1 != odd, second_row, swapped_row)
    low = low_half(WA)

    @pl.loop(0, NOCC // 2)
    def _(big_j):
        lanes = pl.ds(pl.multiple_of(big_j * 128, 128), 128)
        occ_even = occ_ref[slot_ref[2 * big_j]]
        occ_odd = occ_ref[slot_ref[2 * big_j + 1]]
        second = jnp.where(low1, occ_even, occ_odd) - v_second
        second = second - col_ref[...]
        r0 = pl.multiple_of(big_j * 2 * WA, 2 * WA)
        for big_i in range(NOCC // 2):
            tile = slice(big_i * 128, (big_i + 1) * 128)
            s0 = x_ref[pl.ds(r0, WA), tile]
            s1 = x_ref[pl.ds(r0 + WA, WA), tile]
            swaps = (jnp.where(low, s0, pltpu.roll(s1, 64, 1)), jnp.where(low, pltpu.roll(s0, 64, 1), s1))
            for e in range(2):
                i = 2 * big_i + e
                rows = slice(i * WA, (i + 1) * WA)
                value = x_ref[rows, lanes]
                ratio = value / (second + occ_ref[slot_ref[i]])
                t_ref[rows, lanes] = ratio.astype(jnp.bfloat16)
                part = ratio * (2.0 * value - swaps[e])
                z_ref[i : i + 1, lanes] = jnp.sum(part, axis=0, keepdims=True)

    source = lax.broadcasted_iota(jnp.int32, (COLS, 128), 0) // WB
    target = lax.broadcasted_iota(jnp.int32, (COLS, 128), 1) % NOCC
    chooser = jnp.where(source == target, 1.0, 0.0)
    by_pair = jnp.dot(z_ref[...], chooser, preferred_element_type=jnp.float32, precision=lax.Precision.HIGHEST)
    row = lax.broadcasted_iota(jnp.int32, (NOCC, 128), 0) % 8
    lane = lax.broadcasted_iota(jnp.int32, (NOCC, 128), 1) // NOCC
    kept = jnp.where(row == lane, by_pair, 0.0)
    energy_ref[0:1, :] = jnp.sum(kept[:8], axis=0, keepdims=True)
    energy_ref[1:2, :] = jnp.sum(kept[8:], axis=0, keepdims=True)

    @pl.loop(0, COLS // step)
    def _(n):
        lanes = pl.ds(pl.multiple_of(n * step, step), step)
        amp_ref[:, lanes] = jnp.dot(t_ref[...], perm_ref[:, lanes], preferred_element_type=jnp.float32).astype(jnp.bfloat16)


def permutation():
    source = np.arange(COLS)
    target = (source % WB) * NOCC + source // WB
    matrix = np.zeros((COLS, COLS), np.float32)
    matrix[source, target] = 1.0
    return jnp.asarray(matrix, jnp.bfloat16)


def shape(dims, dtype=jnp.bfloat16):
    return jax.ShapeDtypeStruct(dims, dtype)


def per_device(factors, occ_levels, vir_levels, slot_orbital):
    own = factors.reshape(PB, NV)
    a1, a2 = pl.pallas_call(
        prep_kernel,
        out_shape=(shape((ZL * COL, WA // 2, 128)), shape((GRP * ZH, PB // 2, 128))),
        in_specs=[VMEM],
        out_specs=(VMEM, VMEM),
        compiler_params=PARAMS,
    )(own)
    b1 = lax.all_to_all(a1, ("zl", "x", "zh", "k"), 0, 0, tiled=True)
    first = pl.pallas_call(
        first_kernel,
        out_shape=shape((ZL, WA, AUX)),
        in_specs=[VMEM],
        out_specs=VMEM,
        compiler_params=PARAMS,
    )(b1)
    left = lax.all_gather(first.reshape(ZL * WA, AUX), "y", axis=0, tiled=True)
    a2, _ = lax.optimization_barrier((a2, first))
    b2 = lax.all_to_all(a2, ("y", "zl", "zh"), 0, 0, tiled=True)
    second = pl.pallas_call(
        second_kernel,
        out_shape=shape((X, ZH, PB, COLS)),
        in_specs=[VMEM],
        out_specs=VMEM,
        compiler_params=PARAMS,
    )(b2)
    mine = lax.all_to_all(second.reshape(X, ZH * PB, COLS), "x", 0, 0, tiled=True).reshape(AUX // 2, COLS)
    other = lax.ppermute(mine, "k", [(0, 1), (1, 0)])
    amp, energy = pl.pallas_call(
        main_kernel,
        out_shape=(shape((ROWS, COLS)), shape((2, 128), jnp.float32)),
        in_specs=[SMEM, SMEM, VMEM, VMEM, VMEM, VMEM, VMEM],
        out_specs=(VMEM, VMEM),
        scratch_shapes=[
            pltpu.VMEM((ROWS, COLS), jnp.float32),
            pltpu.VMEM((ROWS, COLS), jnp.bfloat16),
            pltpu.VMEM((NOCC, COLS), jnp.float32),
            pltpu.VMEM((WA, 128), jnp.float32),
            pltpu.VMEM((128, 128), jnp.float32),
        ],
        compiler_params=PARAMS,
    )(occ_levels, slot_orbital, vir_levels.reshape(8, 128), left, mine, other, permutation())
    spread = jnp.broadcast_to(energy[None], (ZL * ZH, 2, 128))
    summed = jnp.sum(lax.all_to_all(spread, ("zl", "zh"), 0, 0, tiled=True), axis=0)
    spread = jnp.broadcast_to(summed[None], (Y * X * K, 2, 128))
    summed = jnp.sum(lax.all_to_all(spread, ("y", "x", "k"), 0, 0, tiled=True), axis=0)
    return amp.reshape(NOCC, WA, COLS), summed.reshape(NOCC, NOCC) / (NV * NV)


def solution(mesh):
    fine = Mesh(mesh.devices.reshape(Y, ZL, X, ZH, K), ("y", "zl", "x", "zh", "k"))
    grp, col = ("y", "zl"), ("x", "zh", "k")
    return jax.shard_map(
        per_device,
        mesh=fine,
        in_specs=(P(col, grp, None), P(), P(), P()),
        out_specs=(P(None, col, grp), P()),
        check_vma=False,
    )
```

```python
import functools

import jax
import jax.numpy as jnp
import numpy as np
from jax import lax
from jax.experimental import pallas as pl
from jax.experimental.pallas import tpu as pltpu
from jax.sharding import Mesh, PartitionSpec as P

Y, ZL, X, ZH, K = 8, 2, 4, 4, 2
GRP, COL = Y * ZL, X * ZH * K
AUX, NV, NOCC = 2048, 1024, 16
PB = AUX // COL
WA = NV // COL
WB = NV // GRP
ROWS, COLS = NOCC * WA, NOCC * WB
VMEM = pl.BlockSpec(memory_space=pltpu.VMEM)
SMEM = pl.BlockSpec(memory_space=pltpu.SMEM)
PARAMS = pltpu.CompilerParams(vmem_limit_bytes=48 * 1024 * 1024)


def low_half(rows):
    return lax.broadcasted_iota(jnp.int32, (rows, 128), 1) < 64


def turn(v):
    return pltpu.roll(v.astype(jnp.float32), 64, 1).astype(v.dtype)


def pair_halves(first, second):
    low = low_half(first.shape[0])
    return jnp.where(low, first, turn(second)), jnp.where(low, turn(first), second)


def prep_kernel(x_ref, a1_ref, a2_ref):
    low = low_half(WA // 2)
    for t in range(NV // 128):
        tile = x_ref[:, t * 128 : (t + 1) * 128]
        wide = tile.astype(jnp.float32)
        both = jnp.concatenate([wide, wide], axis=0).T
        for s in range(128 // WA):
            top = both[s * WA : s * WA + WA // 2]
            bottom = both[s * WA + WA // 2 : (s + 1) * WA]
            piece = jnp.where(low, top, bottom).astype(jnp.bfloat16)
            c = t * (128 // WA) + s
            for z in range(ZL):
                a1_ref[z * COL + c] = piece
        even, odd = pair_halves(tile[: PB // 2], tile[PB // 2 :])
        for z in range(ZH):
            a2_ref[(2 * t) * ZH + z] = even
            a2_ref[(2 * t + 1) * ZH + z] = odd


def first_kernel(in_ref, out_ref):
    own = lax.axis_index("k")
    for z in range(ZL):
        for rel in range(K):
            k = own if rel == 0 else 1 - own
            for x in range(X):
                for m in range(ZH // 2):
                    base = z * COL + (x * ZH + 2 * m) * K
                    top, bottom = pair_halves(in_ref[base + k], in_ref[base + K + k])
                    lanes = ((rel * X + x) * ZH + 2 * m) * PB
                    out_ref[z, 0 : WA // 2, lanes : lanes + 128] = top
                    out_ref[z, WA // 2 : WA, lanes : lanes + 128] = bottom


def second_kernel(in_ref, out_ref):
    for z in range(ZH):
        for t in range(NOCC // 2):
            top, bottom = pair_halves(in_ref[(2 * t) * ZH + z], in_ref[(2 * t + 1) * ZH + z])
            for copy in range(X):
                out_ref[copy, z, 0 : PB // 2, t * 128 : (t + 1) * 128] = top
                out_ref[copy, z, PB // 2 : PB, t * 128 : (t + 1) * 128] = bottom


def inverse_kernel(occ_ref, slot_ref, vir_ref, inv_ref, col_ref, v_ref):
    column = (lax.axis_index("x") * ZH + lax.axis_index("zh")) * K + lax.axis_index("k")
    group = lax.axis_index("y") * ZL + lax.axis_index("zl")
    first_row = vir_ref[pl.ds(column // 4, 1), :]
    v_ref[...] = jnp.broadcast_to(first_row, (128, 128)).T
    col_ref[...] = v_ref[pl.ds(pl.multiple_of((column % 4) * WA, WA), WA), :]
    second_row = vir_ref[pl.ds(group // 2, 1), :]
    low1 = lax.broadcasted_iota(jnp.int32, (1, 128), 1) < 64
    swapped_row = pltpu.roll(jnp.broadcast_to(second_row, (8, 128)), 64, 1)[:1]
    odd = group % 2 == 1
    v_second = jnp.where(low1 != odd, second_row, swapped_row)

    @pl.loop(0, NOCC // 2)
    def _(big_j):
        lanes = pl.ds(pl.multiple_of(big_j * 128, 128), 128)
        occ_even = occ_ref[slot_ref[2 * big_j]]
        occ_odd = occ_ref[slot_ref[2 * big_j + 1]]
        second = jnp.where(low1, occ_even, occ_odd) - v_second - col_ref[...]
        for i in range(NOCC):
            inv_ref[i * WA : (i + 1) * WA, lanes] = 1.0 / (second + occ_ref[slot_ref[i]])


def main_kernel(l_ref, r0_ref, r1_ref, inv_ref, amp_ref, energy_ref, x_ref, z_ref):
    half = AUX // 2
    step = 256

    @pl.loop(0, COLS // step)
    def _(n):
        lanes = pl.ds(pl.multiple_of(n * step, step), step)
        x_ref[:, lanes] = jnp.dot(l_ref[:, :half], r0_ref[:, lanes], preferred_element_type=jnp.float32) + jnp.dot(
            l_ref[:, half:], r1_ref[:, lanes], preferred_element_type=jnp.float32
        )

    low = low_half(WA)

    @pl.loop(0, NOCC // 2)
    def _(big_j):
        lanes = pl.ds(pl.multiple_of(big_j * 128, 128), 128)
        r0 = pl.multiple_of(big_j * 2 * WA, 2 * WA)
        for big_i in range(NOCC // 2):
            tile = slice(big_i * 128, (big_i + 1) * 128)
            s0 = x_ref[pl.ds(r0, WA), tile]
            s1 = x_ref[pl.ds(r0 + WA, WA), tile]
            swaps = (jnp.where(low, s0, pltpu.roll(s1, 64, 1)), jnp.where(low, pltpu.roll(s0, 64, 1), s1))
            for e in range(2):
                i = 2 * big_i + e
                rows = slice(i * WA, (i + 1) * WA)
                value = x_ref[rows, lanes]
                ratio = value * inv_ref[rows, lanes]
                amp_ref[rows, lanes] = ratio.astype(jnp.bfloat16)
                part = ratio * (2.0 * value - swaps[e])
                z_ref[i : i + 1, lanes] = jnp.sum(part, axis=0, keepdims=True)

    source = lax.broadcasted_iota(jnp.int32, (COLS, 128), 0) // WB
    target = lax.broadcasted_iota(jnp.int32, (COLS, 128), 1) % NOCC
    chooser = jnp.where(source == target, 1.0, 0.0)
    by_pair = jnp.dot(z_ref[...], chooser, preferred_element_type=jnp.float32, precision=lax.Precision.HIGHEST)
    row = lax.broadcasted_iota(jnp.int32, (NOCC, 128), 0) % 8
    lane = lax.broadcasted_iota(jnp.int32, (NOCC, 128), 1) // NOCC
    kept = jnp.where(row == lane, by_pair, 0.0)
    energy_ref[0:1, :] = jnp.sum(kept[:8], axis=0, keepdims=True)
    energy_ref[1:2, :] = jnp.sum(kept[8:], axis=0, keepdims=True)


def order_kernel(t_ref, perm_ref, amp_ref):
    step = 256

    @pl.loop(0, COLS // step)
    def _(n):
        lanes = pl.ds(pl.multiple_of(n * step, step), step)
        amp_ref[:, lanes] = jnp.dot(t_ref[...], perm_ref[:, lanes], preferred_element_type=jnp.float32).astype(jnp.bfloat16)


def permutation():
    source = np.arange(COLS)
    target = (source % WB) * NOCC + source // WB
    matrix = np.zeros((COLS, COLS), np.float32)
    matrix[source, target] = 1.0
    return jnp.asarray(matrix, jnp.bfloat16)


def shape(dims, dtype=jnp.bfloat16):
    return jax.ShapeDtypeStruct(dims, dtype)


def per_device(factors, occ_levels, vir_levels, slot_orbital):
    own = factors.reshape(PB, NV)
    a1, a2 = pl.pallas_call(
        prep_kernel,
        out_shape=(shape((ZL * COL, WA // 2, 128)), shape((GRP * ZH, PB // 2, 128))),
        in_specs=[VMEM],
        out_specs=(VMEM, VMEM),
        compiler_params=PARAMS,
    )(own)
    b1 = lax.all_to_all(a1, ("zl", "x", "zh", "k"), 0, 0, tiled=True)
    first = pl.pallas_call(
        first_kernel,
        out_shape=shape((ZL, WA, AUX)),
        in_specs=[VMEM],
        out_specs=VMEM,
        compiler_params=PARAMS,
    )(b1)
    left = lax.all_gather(first.reshape(ZL * WA, AUX), "y", axis=0, tiled=True)
    a2, _ = lax.optimization_barrier((a2, first))
    b2 = lax.all_to_all(a2, ("y", "zl", "zh"), 0, 0, tiled=True)
    second = pl.pallas_call(
        second_kernel,
        out_shape=shape((X, ZH, PB, COLS)),
        in_specs=[VMEM],
        out_specs=VMEM,
        compiler_params=PARAMS,
    )(b2)
    mine = lax.all_to_all(second.reshape(X, ZH * PB, COLS), "x", 0, 0, tiled=True).reshape(AUX // 2, COLS)
    mine, left = lax.optimization_barrier((mine, left))
    other = lax.ppermute(mine, "k", [(0, 1), (1, 0)])
    inverse = pl.pallas_call(
        inverse_kernel,
        out_shape=shape((ROWS, COLS), jnp.float32),
        in_specs=[SMEM, SMEM, VMEM],
        out_specs=VMEM,
        scratch_shapes=[pltpu.VMEM((WA, 128), jnp.float32), pltpu.VMEM((128, 128), jnp.float32)],
        compiler_params=PARAMS,
        cost_estimate=pl.CostEstimate(flops=ROWS * COLS * 10, bytes_accessed=4 * ROWS * COLS * 4, transcendentals=0),
    )(occ_levels, slot_orbital, vir_levels.reshape(8, 128))
    ratio, energy = pl.pallas_call(
        main_kernel,
        out_shape=(shape((ROWS, COLS)), shape((2, 128), jnp.float32)),
        in_specs=[VMEM, VMEM, VMEM, VMEM],
        out_specs=(VMEM, VMEM),
        scratch_shapes=[pltpu.VMEM((ROWS, COLS), jnp.float32), pltpu.VMEM((NOCC, COLS), jnp.float32)],
        compiler_params=PARAMS,
    )(left, mine, other, inverse)
    amp = pl.pallas_call(
        order_kernel,
        out_shape=shape((ROWS, COLS)),
        in_specs=[VMEM, VMEM],
        out_specs=VMEM,
        compiler_params=PARAMS,
        cost_estimate=pl.CostEstimate(flops=2 * ROWS * COLS * COLS, bytes_accessed=2 * COLS * COLS + 4 * ROWS * COLS, transcendentals=0),
    )(ratio, permutation())
    spread = jnp.broadcast_to(energy[None], (ZL * ZH, 2, 128))
    summed = jnp.sum(lax.all_to_all(spread, ("zl", "zh"), 0, 0, tiled=True), axis=0)
    spread = jnp.broadcast_to(summed[None], (Y * X * K, 2, 128))
    summed = jnp.sum(lax.all_to_all(spread, ("y", "x", "k"), 0, 0, tiled=True), axis=0)
    return amp.reshape(NOCC, WA, COLS), summed.reshape(NOCC, NOCC) / (NV * NV)


def solution(mesh):
    fine = Mesh(mesh.devices.reshape(Y, ZL, X, ZH, K), ("y", "zl", "x", "zh", "k"))
    grp, col = ("y", "zl"), ("x", "zh", "k")
    return jax.shard_map(
        per_device,
        mesh=fine,
        in_specs=(P(col, grp, None), P(), P(), P()),
        out_specs=(P(None, col, grp), P()),
        check_vma=False,
    )
```

```python
import jax
import jax.numpy as jnp
import numpy as np
from jax import lax
from jax.experimental import pallas as pl
from jax.experimental.pallas import tpu as pltpu
from jax.sharding import Mesh, PartitionSpec as P

Y, ZL, X, ZH, K = 8, 2, 4, 4, 2
GRP, COL = Y * ZL, X * ZH * K
AUX, NV, NOCC = 2048, 1024, 16
PB = AUX // COL
WA = NV // COL
WB = NV // GRP
ROWS, COLS = NOCC * WA, NOCC * WB
STEP = 256
VMEM = pl.BlockSpec(memory_space=pltpu.VMEM)
SMEM = pl.BlockSpec(memory_space=pltpu.SMEM)
PARAMS = pltpu.CompilerParams(vmem_limit_bytes=16 * 1024 * 1024)


def low_half(rows):
    return lax.broadcasted_iota(jnp.int32, (rows, 128), 1) < 64


def turn(v):
    return pltpu.roll(v.astype(jnp.float32), 64, 1).astype(v.dtype)


def pair_halves(first, second):
    low = low_half(first.shape[0])
    return jnp.where(low, first, turn(second)), jnp.where(low, turn(first), second)


def prep_kernel(x_ref, a1_ref, a2_ref):
    low = low_half(WA // 2)
    for t in range(NV // 128):
        tile = x_ref[:, t * 128 : (t + 1) * 128]
        wide = tile.astype(jnp.float32)
        both = jnp.concatenate([wide, wide], axis=0).T
        for s in range(128 // WA):
            top = both[s * WA : s * WA + WA // 2]
            bottom = both[s * WA + WA // 2 : (s + 1) * WA]
            piece = jnp.where(low, top, bottom).astype(jnp.bfloat16)
            c = t * (128 // WA) + s
            for z in range(ZL):
                a1_ref[z * COL + c] = piece
        even, odd = pair_halves(tile[: PB // 2], tile[PB // 2 :])
        a2_ref[2 * t] = even
        a2_ref[2 * t + 1] = odd


def first_kernel(in_ref, out_ref):
    own = lax.axis_index("k")
    for z in range(ZL):
        for rel in range(K):
            k = own if rel == 0 else 1 - own
            for x in range(X):
                for m in range(ZH // 2):
                    base = z * COL + (x * ZH + 2 * m) * K
                    top, bottom = pair_halves(in_ref[base + k], in_ref[base + K + k])
                    lanes = ((rel * X + x) * ZH + 2 * m) * PB
                    out_ref[z, 0 : WA // 2, lanes : lanes + 128] = top
                    out_ref[z, WA // 2 : WA, lanes : lanes + 128] = bottom


def second_kernel(in_ref, out_ref):
    for t in range(NOCC // 2):
        top, bottom = pair_halves(in_ref[2 * t], in_ref[2 * t + 1])
        out_ref[0 : PB // 2, t * 128 : (t + 1) * 128] = top
        out_ref[PB // 2 : PB, t * 128 : (t + 1) * 128] = bottom


def inverse_kernel(occ_ref, slot_ref, vir_ref, inv_ref, col_ref, v_ref):
    column = (lax.axis_index("x") * ZH + lax.axis_index("zh")) * K + lax.axis_index("k")
    group = lax.axis_index("y") * ZL + lax.axis_index("zl")
    first_row = vir_ref[pl.ds(column // 4, 1), :]
    v_ref[...] = jnp.broadcast_to(first_row, (128, 128)).T
    col_ref[...] = v_ref[pl.ds(pl.multiple_of((column % 4) * WA, WA), WA), :]
    second_row = vir_ref[pl.ds(group // 2, 1), :]
    low1 = lax.broadcasted_iota(jnp.int32, (1, 128), 1) < 64
    swapped_row = pltpu.roll(jnp.broadcast_to(second_row, (8, 128)), 64, 1)[:1]
    odd = group % 2 == 1
    v_second = jnp.where(low1 != odd, second_row, swapped_row)

    @pl.loop(0, NOCC // 2)
    def _(big_j):
        lanes = pl.ds(pl.multiple_of(big_j * 128, 128), 128)
        occ_even = occ_ref[slot_ref[2 * big_j]]
        occ_odd = occ_ref[slot_ref[2 * big_j + 1]]
        second = jnp.where(low1, occ_even, occ_odd) - v_second - col_ref[...]
        for i in range(NOCC):
            inv_ref[i * WA : (i + 1) * WA, lanes] = 1.0 / (second + occ_ref[slot_ref[i]])


def half_kernel(l_ref, r_ref, x_ref):
    @pl.loop(0, COLS // STEP)
    def _(n):
        lanes = pl.ds(pl.multiple_of(n * STEP, STEP), STEP)
        x_ref[:, lanes] = jnp.dot(l_ref[:, : AUX // 2], r_ref[:, lanes], preferred_element_type=jnp.float32)


def main_kernel(half_ref, l_ref, r_ref, inv_ref, amp_ref, energy_ref, x_ref, z_ref):
    @pl.loop(0, COLS // STEP)
    def _(n):
        lanes = pl.ds(pl.multiple_of(n * STEP, STEP), STEP)
        x_ref[:, lanes] = half_ref[:, lanes] + jnp.dot(l_ref[:, AUX // 2 :], r_ref[:, lanes], preferred_element_type=jnp.float32)

    low = low_half(WA)

    @pl.loop(0, NOCC // 2)
    def _(big_j):
        lanes = pl.ds(pl.multiple_of(big_j * 128, 128), 128)
        r0 = pl.multiple_of(big_j * 2 * WA, 2 * WA)
        for big_i in range(NOCC // 2):
            tile = slice(big_i * 128, (big_i + 1) * 128)
            s0 = x_ref[pl.ds(r0, WA), tile]
            s1 = x_ref[pl.ds(r0 + WA, WA), tile]
            swaps = (jnp.where(low, s0, pltpu.roll(s1, 64, 1)), jnp.where(low, pltpu.roll(s0, 64, 1), s1))
            for e in range(2):
                i = 2 * big_i + e
                rows = slice(i * WA, (i + 1) * WA)
                value = x_ref[rows, lanes]
                ratio = value * inv_ref[rows, lanes]
                amp_ref[rows, lanes] = ratio.astype(jnp.bfloat16)
                part = ratio * (2.0 * value - swaps[e])
                z_ref[i * 8 : (i + 1) * 8, lanes] = jnp.sum(part.reshape(WA // 8, 8, 128), axis=0)

    source = lax.broadcasted_iota(jnp.int32, (COLS, 128), 0) // WB
    target = lax.broadcasted_iota(jnp.int32, (COLS, 128), 1) % NOCC
    chooser = jnp.where(source == target, 1.0, 0.0)
    by_pair = jnp.dot(z_ref[...], chooser, preferred_element_type=jnp.float32, precision=lax.Precision.HIGHEST)
    row = (lax.broadcasted_iota(jnp.int32, (NOCC * 8, 128), 0) // 8) % 8
    lane = lax.broadcasted_iota(jnp.int32, (NOCC * 8, 128), 1) // NOCC
    kept = jnp.where(row == lane, by_pair, 0.0)
    halves = [jnp.sum(kept[h * 64 : (h + 1) * 64], axis=0, keepdims=True) for h in range(2)]
    energy = jnp.concatenate(halves, axis=0)
    for z in range(ZL * ZH):
        energy_ref[z] = energy


def middle_kernel(in_ref, out_ref):
    total = jnp.sum(in_ref[...], axis=0)
    for n in range(Y * X * K):
        out_ref[n] = total


def last_kernel(in_ref, out_ref):
    total = jnp.sum(in_ref[...], axis=0) * (1.0 / (NV * NV))
    rows = jnp.concatenate([jnp.broadcast_to(total[h : h + 1], (8, 128)) for h in range(2)], axis=0)
    row = lax.broadcasted_iota(jnp.int32, (NOCC, 128), 0) % 8
    lane = lax.broadcasted_iota(jnp.int32, (NOCC, 128), 1) // NOCC
    kept = jnp.where(row == lane, rows, 0.0)
    source = lax.broadcasted_iota(jnp.int32, (128, NOCC), 0) % NOCC
    target = lax.broadcasted_iota(jnp.int32, (128, NOCC), 1)
    chooser = jnp.where(source == target, 1.0, 0.0)
    out_ref[...] = jnp.dot(kept, chooser, preferred_element_type=jnp.float32, precision=lax.Precision.HIGHEST)


def order_kernel(t_ref, perm_ref, amp_ref):
    @pl.loop(0, COLS // STEP)
    def _(n):
        lanes = pl.ds(pl.multiple_of(n * STEP, STEP), STEP)
        amp_ref[:, lanes] = jnp.dot(t_ref[...], perm_ref[:, lanes], preferred_element_type=jnp.float32).astype(jnp.bfloat16)


def permutation():
    source = np.arange(COLS)
    target = (source % WB) * NOCC + source // WB
    matrix = np.zeros((COLS, COLS), np.float32)
    matrix[source, target] = 1.0
    return jnp.asarray(matrix, jnp.bfloat16)


def shape(dims, dtype=jnp.bfloat16):
    return jax.ShapeDtypeStruct(dims, dtype)


def call(kernel, out_shape, operands, in_specs=None, scratch=(), flops=0):
    kinds = in_specs or [VMEM] * len(operands)
    cost = pl.CostEstimate(flops=flops, bytes_accessed=4 * ROWS * COLS, transcendentals=0) if flops else None
    return pl.pallas_call(
        kernel,
        out_shape=out_shape,
        in_specs=kinds,
        out_specs=jax.tree.map(lambda _: VMEM, out_shape),
        scratch_shapes=scratch,
        compiler_params=PARAMS,
        cost_estimate=cost,
    )(*operands)


def per_device(factors, occ_levels, vir_levels, slot_orbital):
    f32 = jnp.float32
    a1, a2 = call(
        prep_kernel,
        (shape((ZL * COL, WA // 2, 128)), shape((GRP, PB // 2, 128))),
        [factors.reshape(PB, NV)],
    )
    b1 = lax.all_to_all(a1, ("zl", "x", "zh", "k"), 0, 0, tiled=True)
    first = call(first_kernel, shape((ZL, WA, AUX)), [b1])
    left = lax.all_gather(first.reshape(ZL * WA, AUX), "y", axis=0, tiled=True)
    a2, _ = lax.optimization_barrier((a2, first))
    b2 = lax.all_to_all(a2, ("y", "zl"), 0, 0, tiled=True)
    second = call(second_kernel, shape((PB, COLS)), [b2])
    second = lax.all_gather(second, "zh", axis=0, tiled=True)
    spread = jnp.broadcast_to(second[None], (X, ZH * PB, COLS))
    mine = lax.all_to_all(spread, "x", 0, 0, tiled=True).reshape(AUX // 2, COLS)
    mine, left = lax.optimization_barrier((mine, left))
    other = lax.ppermute(mine, "k", [(0, 1), (1, 0)])
    inverse = call(
        inverse_kernel,
        shape((ROWS, COLS), f32),
        [occ_levels, slot_orbital, vir_levels.reshape(8, 128)],
        in_specs=[SMEM, SMEM, VMEM],
        scratch=[pltpu.VMEM((WA, 128), f32), pltpu.VMEM((128, 128), f32)],
        flops=ROWS * COLS * 10,
    )
    half = call(half_kernel, shape((ROWS, COLS), f32), [left, mine], flops=ROWS * COLS * AUX)
    ratio, energy = call(
        main_kernel,
        (shape((ROWS, COLS)), shape((ZL * ZH, 2, 128), f32)),
        [half, left, other, inverse],
        scratch=[pltpu.VMEM((ROWS, COLS), f32), pltpu.VMEM((NOCC * 8, COLS), f32)],
    )
    amp = call(order_kernel, shape((ROWS, COLS)), [ratio, permutation()], flops=2 * ROWS * COLS * COLS)
    energy = lax.all_to_all(energy, ("zl", "zh"), 0, 0, tiled=True)
    energy = call(middle_kernel, shape((Y * X * K, 2, 128), f32), [energy])
    energy = lax.all_to_all(energy, ("y", "x", "k"), 0, 0, tiled=True)
    return amp.reshape(NOCC, WA, COLS), call(last_kernel, shape((NOCC, NOCC), f32), [energy])


def solution(mesh):
    fine = Mesh(mesh.devices.reshape(Y, ZL, X, ZH, K), ("y", "zl", "x", "zh", "k"))
    grp, col = ("y", "zl"), ("x", "zh", "k")
    return jax.shard_map(
        per_device,
        mesh=fine,
        in_specs=(P(col, grp, None), P(), P(), P()),
        out_specs=(P(None, col, grp), P()),
        check_vma=False,
    )
```

```python
import jax
import jax.numpy as jnp
import numpy as np
from jax import lax
from jax.experimental import pallas as pl
from jax.experimental.pallas import tpu as pltpu
from jax.sharding import Mesh, PartitionSpec as P

Y, ZL, X, ZH, K = 8, 2, 4, 4, 2
GRP, COL = Y * ZL, X * ZH * K
AUX, NV, NOCC = 2048, 1024, 16
PB = AUX // COL
WA = NV // COL
WB = NV // GRP
ROWS, COLS = NOCC * WA, NOCC * WB
STEP = 256
VMEM = pl.BlockSpec(memory_space=pltpu.VMEM)
SMEM = pl.BlockSpec(memory_space=pltpu.SMEM)
PARAMS = pltpu.CompilerParams(vmem_limit_bytes=16 * 1024 * 1024)


def low_half(rows):
    return lax.broadcasted_iota(jnp.int32, (rows, 128), 1) < 64


def turn(v):
    return pltpu.roll(v.astype(jnp.float32), 64, 1).astype(v.dtype)


def pair_halves(first, second):
    low = low_half(first.shape[0])
    return jnp.where(low, first, turn(second)), jnp.where(low, turn(first), second)


def prep_kernel(x_ref, a1_ref, a2_ref):
    low = low_half(WA // 2)
    for t in range(NV // 128):
        tile = x_ref[:, t * 128 : (t + 1) * 128]
        wide = tile.astype(jnp.float32)
        both = jnp.concatenate([wide, wide], axis=0).T
        for s in range(128 // WA):
            top = both[s * WA : s * WA + WA // 2]
            bottom = both[s * WA + WA // 2 : (s + 1) * WA]
            piece = jnp.where(low, top, bottom).astype(jnp.bfloat16)
            c = t * (128 // WA) + s
            for z in range(ZL):
                a1_ref[z * COL + c] = piece
        even, odd = pair_halves(tile[: PB // 2], tile[PB // 2 :])
        a2_ref[2 * t] = even
        a2_ref[2 * t + 1] = odd


def first_kernel(in_ref, out_ref):
    own = lax.axis_index("k")
    for z in range(ZL):
        for rel in range(K):
            k = own if rel == 0 else 1 - own
            for x in range(X):
                for m in range(ZH // 2):
                    base = z * COL + (x * ZH + 2 * m) * K
                    top, bottom = pair_halves(in_ref[base + k], in_ref[base + K + k])
                    lanes = ((rel * X + x) * ZH + 2 * m) * PB
                    out_ref[z, 0 : WA // 2, lanes : lanes + 128] = top
                    out_ref[z, WA // 2 : WA, lanes : lanes + 128] = bottom


def second_kernel(in_ref, out_ref):
    for t in range(NOCC // 2):
        top, bottom = pair_halves(in_ref[2 * t], in_ref[2 * t + 1])
        out_ref[0 : PB // 2, t * 128 : (t + 1) * 128] = top
        out_ref[PB // 2 : PB, t * 128 : (t + 1) * 128] = bottom


def inverse_kernel(occ_ref, slot_ref, vir_ref, inv_ref, col_ref, v_ref):
    column = (lax.axis_index("x") * ZH + lax.axis_index("zh")) * K + lax.axis_index("k")
    group = lax.axis_index("y") * ZL + lax.axis_index("zl")
    first_row = vir_ref[pl.ds(column // 4, 1), :]
    v_ref[...] = jnp.broadcast_to(first_row, (128, 128)).T
    col_ref[...] = v_ref[pl.ds(pl.multiple_of((column % 4) * WA, WA), WA), :]
    second_row = vir_ref[pl.ds(group // 2, 1), :]
    low1 = lax.broadcasted_iota(jnp.int32, (1, 128), 1) < 64
    swapped_row = pltpu.roll(jnp.broadcast_to(second_row, (8, 128)), 64, 1)[:1]
    odd = group % 2 == 1
    v_second = jnp.where(low1 != odd, second_row, swapped_row)

    @pl.loop(0, NOCC // 2)
    def _(big_j):
        lanes = pl.ds(pl.multiple_of(big_j * 128, 128), 128)
        occ_even = occ_ref[slot_ref[2 * big_j]]
        occ_odd = occ_ref[slot_ref[2 * big_j + 1]]
        second = jnp.where(low1, occ_even, occ_odd) - v_second - col_ref[...]
        for i in range(NOCC):
            inv_ref[i * WA : (i + 1) * WA, lanes] = 1.0 / (second + occ_ref[slot_ref[i]])


def half_kernel(l_ref, r_ref, x_ref):
    @pl.loop(0, COLS // STEP)
    def _(n):
        lanes = pl.ds(pl.multiple_of(n * STEP, STEP), STEP)
        x_ref[:, lanes] = jnp.dot(l_ref[:, : AUX // 2], r_ref[:, lanes], preferred_element_type=jnp.float32)


def main_kernel(half_ref, l_ref, r_ref, inv_ref, amp_ref, energy_ref, x_ref, z_ref):
    low = low_half(WA)
    tiles = COLS // 128
    z_ref[...] = jnp.zeros_like(z_ref)

    def at(i, tile):
        return slice(i * WA, (i + 1) * WA), slice(tile * 128, (tile + 1) * 128)

    def product(n):
        lanes = slice(n * STEP, (n + 1) * STEP)
        x_ref[:, lanes] = half_ref[:, lanes] + jnp.dot(l_ref[:, AUX // 2 :], r_ref[:, lanes], preferred_element_type=jnp.float32)

    def ratios(big_i, big_j):
        if big_i <= big_j:
            s0 = x_ref[at(2 * big_j, big_i)]
            s1 = x_ref[at(2 * big_j + 1, big_i)]
            swaps = (jnp.where(low, s0, pltpu.roll(s1, 64, 1)), jnp.where(low, pltpu.roll(s0, 64, 1), s1))
        for e in range(2):
            i = 2 * big_i + e
            value = x_ref[at(i, big_j)]
            ratio = value * inv_ref[at(i, big_j)]
            amp_ref[at(i, big_j)] = ratio.astype(jnp.bfloat16)
            if big_i <= big_j:
                part = ratio * (2.0 * value - swaps[e])
                z_ref[i * 8 : (i + 1) * 8, big_j * 128 : (big_j + 1) * 128] = jnp.sum(part.reshape(WA // 8, 8, 128), axis=0)

    def finish(n):
        width = STEP // 128
        for new in range(n * width, (n + 1) * width):
            for old in range(new + 1):
                ratios(old, new)
                if old < new:
                    ratios(new, old)

    product(0)
    for n in range(1, COLS // STEP):
        product(n)
        finish(n - 1)
    finish(COLS // STEP - 1)

    source = lax.broadcasted_iota(jnp.int32, (COLS, 128), 0) // WB
    target = lax.broadcasted_iota(jnp.int32, (COLS, 128), 1) % NOCC
    chooser = jnp.where(source == target, 1.0, 0.0)
    by_pair = jnp.dot(z_ref[...], chooser, preferred_element_type=jnp.float32, precision=lax.Precision.HIGHEST)
    row = (lax.broadcasted_iota(jnp.int32, (NOCC * 8, 128), 0) // 8) % 8
    lane = lax.broadcasted_iota(jnp.int32, (NOCC * 8, 128), 1) // NOCC
    kept = jnp.where(row == lane, by_pair, 0.0)
    halves = [jnp.sum(kept[h * 64 : (h + 1) * 64], axis=0, keepdims=True) for h in range(2)]
    energy = jnp.concatenate(halves, axis=0)
    for z in range(ZL * ZH * K):
        energy_ref[z] = energy


def middle_kernel(in_ref, out_ref):
    total = jnp.sum(in_ref[...], axis=0)
    for n in range(Y * X):
        out_ref[n] = total


def last_kernel(in_ref, out_ref):
    total = jnp.sum(in_ref[...], axis=0) * (1.0 / (NV * NV))
    rows = jnp.concatenate([jnp.broadcast_to(total[h : h + 1], (8, 128)) for h in range(2)], axis=0)
    row = lax.broadcasted_iota(jnp.int32, (NOCC, 128), 0) % 8
    lane = lax.broadcasted_iota(jnp.int32, (NOCC, 128), 1) // NOCC
    kept = jnp.where(row == lane, rows, 0.0)
    source = lax.broadcasted_iota(jnp.int32, (128, NOCC), 0) % NOCC
    target = lax.broadcasted_iota(jnp.int32, (128, NOCC), 1)
    chooser = jnp.where(source == target, 1.0, 0.0)
    exact = dict(preferred_element_type=jnp.float32, precision=lax.Precision.HIGHEST)
    upper = jnp.dot(kept, chooser, **exact)
    mirror = lax.dot_general(chooser, kept, (((0,), (1,)), ((), ())), **exact)
    i = lax.broadcasted_iota(jnp.int32, (NOCC, NOCC), 0)
    j = lax.broadcasted_iota(jnp.int32, (NOCC, NOCC), 1)
    out_ref[...] = jnp.where(i <= j, upper, mirror)


def order_kernel(t_ref, perm_ref, amp_ref, buf_ref, sems):
    copies = []
    for n in range(COLS // STEP):
        lanes = slice(n * STEP, (n + 1) * STEP)
        buf_ref[:, lanes] = jnp.dot(t_ref[...], perm_ref[:, lanes], preferred_element_type=jnp.float32).astype(jnp.bfloat16)
        copies.append(pltpu.make_async_copy(buf_ref.at[:, lanes], amp_ref.at[:, lanes], sems.at[n]))
        copies[-1].start()
    for copy in copies:
        copy.wait()


def permutation():
    source = np.arange(COLS)
    target = (source % WB) * NOCC + source // WB
    matrix = np.zeros((COLS, COLS), np.float32)
    matrix[source, target] = 1.0
    return jnp.asarray(matrix, jnp.bfloat16)


def shape(dims, dtype=jnp.bfloat16):
    return jax.ShapeDtypeStruct(dims, dtype)


def call(kernel, out_shape, operands, in_specs=None, scratch=(), flops=0, out=VMEM):
    kinds = in_specs or [VMEM] * len(operands)
    cost = pl.CostEstimate(flops=flops, bytes_accessed=4 * ROWS * COLS, transcendentals=0) if flops else None
    return pl.pallas_call(
        kernel,
        out_shape=out_shape,
        in_specs=kinds,
        out_specs=jax.tree.map(lambda _: out, out_shape),
        scratch_shapes=scratch,
        compiler_params=PARAMS,
        cost_estimate=cost,
    )(*operands)


def per_device(factors, occ_levels, vir_levels, slot_orbital):
    f32 = jnp.float32
    a1, a2 = call(
        prep_kernel,
        (shape((ZL * COL, WA // 2, 128)), shape((GRP, PB // 2, 128))),
        [factors.reshape(PB, NV)],
    )
    b1 = lax.all_to_all(a1, ("zl", "x", "zh", "k"), 0, 0, tiled=True)
    first = call(first_kernel, shape((ZL, WA, AUX)), [b1])
    left = lax.all_gather(first.reshape(ZL * WA, AUX), "y", axis=0, tiled=True)
    a2, _ = lax.optimization_barrier((a2, first))
    b2 = lax.all_to_all(a2, ("y", "zl"), 0, 0, tiled=True)
    second = call(second_kernel, shape((PB, COLS)), [b2])
    second = lax.all_gather(second, "zh", axis=0, tiled=True)
    spread = jnp.broadcast_to(second[None], (X, ZH * PB, COLS))
    mine = lax.all_to_all(spread, "x", 0, 0, tiled=True).reshape(AUX // 2, COLS)
    mine, left = lax.optimization_barrier((mine, left))
    other = lax.ppermute(mine, "k", [(0, 1), (1, 0)])
    inverse = call(
        inverse_kernel,
        shape((ROWS, COLS), f32),
        [occ_levels, slot_orbital, vir_levels.reshape(8, 128)],
        in_specs=[SMEM, SMEM, VMEM],
        scratch=[pltpu.VMEM((WA, 128), f32), pltpu.VMEM((128, 128), f32)],
        flops=ROWS * COLS * 10,
    )
    half = call(half_kernel, shape((ROWS, COLS), f32), [left, mine], flops=ROWS * COLS * AUX)
    ratio, energy = call(
        main_kernel,
        (shape((ROWS, COLS)), shape((ZL * ZH * K, 2, 128), f32)),
        [half, left, other, inverse],
        scratch=[pltpu.VMEM((ROWS, COLS), f32), pltpu.VMEM((NOCC * 8, COLS), f32)],
    )
    amp = call(
        order_kernel,
        shape((ROWS, COLS)),
        [ratio, permutation()],
        scratch=[pltpu.VMEM((ROWS, COLS), jnp.bfloat16), pltpu.SemaphoreType.DMA((COLS // STEP,))],
        flops=2 * ROWS * COLS * COLS,
        out=pl.BlockSpec(memory_space=pl.ANY),
    )
    energy = lax.all_to_all(energy, ("zl", "zh", "k"), 0, 0, tiled=True)
    energy = call(middle_kernel, shape((Y * X, 2, 128), f32), [energy])
    energy = lax.all_to_all(energy, ("y", "x"), 0, 0, tiled=True)
    return amp.reshape(NOCC, WA, COLS), call(last_kernel, shape((NOCC, NOCC), f32), [energy])


def solution(mesh):
    fine = Mesh(mesh.devices.reshape(Y, ZL, X, ZH, K), ("y", "zl", "x", "zh", "k"))
    grp, col = ("y", "zl"), ("x", "zh", "k")
    return jax.shard_map(
        per_device,
        mesh=fine,
        in_specs=(P(col, grp, None), P(), P(), P()),
        out_specs=(P(None, col, grp), P()),
        check_vma=False,
    )
```

```python
import jax
import jax.numpy as jnp
import numpy as np
from jax import lax
from jax.experimental import pallas as pl
from jax.experimental.pallas import tpu as pltpu
from jax.sharding import Mesh, PartitionSpec as P

Y, ZL, X, ZH, K = 8, 2, 4, 4, 2
GRP, COL = Y * ZL, X * ZH * K
AUX, NV, NOCC = 2048, 1024, 16
PB = AUX // COL
WA = NV // COL
WB = NV // GRP
ROWS, COLS = NOCC * WA, NOCC * WB
STEP = 256
CHUNK = ZH * PB
ARRIVAL = tuple((d, rel) for d in (0, 1, 3, 2) for rel in range(K))
GROUP = 2 * CHUNK
VMEM = pl.BlockSpec(memory_space=pltpu.VMEM)
SMEM = pl.BlockSpec(memory_space=pltpu.SMEM)
ANY = pl.BlockSpec(memory_space=pl.ANY)


def low_half(rows):
    return lax.broadcasted_iota(jnp.int32, (rows, 128), 1) < 64


def turn(v):
    return pltpu.roll(v.astype(jnp.float32), 64, 1).astype(v.dtype)


def pair_halves(first, second):
    low = low_half(first.shape[0])
    return jnp.where(low, first, turn(second)), jnp.where(low, turn(first), second)


def prep_kernel(x_ref, a1_ref, a2_ref):
    low = low_half(WA // 2)
    for t in range(NV // 128):
        tile = x_ref[:, t * 128 : (t + 1) * 128]
        wide = tile.astype(jnp.float32)
        both = jnp.concatenate([wide, wide], axis=0).T
        for s in range(128 // WA):
            top = both[s * WA : s * WA + WA // 2]
            bottom = both[s * WA + WA // 2 : (s + 1) * WA]
            piece = jnp.where(low, top, bottom).astype(jnp.bfloat16)
            c = t * (128 // WA) + s
            a1_ref[c] = piece
        even, odd = pair_halves(tile[: PB // 2], tile[PB // 2 :])
        a2_ref[2 * t] = even
        a2_ref[2 * t + 1] = odd


def first_kernel(in_ref, out_ref):
    own_k, own_x = lax.axis_index("k"), lax.axis_index("x")
    for n, (d, rel) in enumerate(ARRIVAL):
        k = (own_k + rel) % K
        x = (own_x + X - d) % X
        for m in range(ZH // 2):
            base = (x * ZH + 2 * m) * K + k
            top, bottom = pair_halves(in_ref[base], in_ref[base + K])
            lanes = (n * ZH + 2 * m) * PB
            for y in range(Y):
                out_ref[y, 0 : WA // 2, lanes : lanes + 128] = top
                out_ref[y, WA // 2 : WA, lanes : lanes + 128] = bottom


def place_kernel(own_ref, near_ref, out_ref):
    zl = lax.axis_index("zl")
    for y in range(Y):
        out_ref[y, zl] = own_ref[y]
        out_ref[y, 1 - zl] = near_ref[y]


def second_kernel(in_ref, out_ref):
    for t in range(NOCC // 2):
        top, bottom = pair_halves(in_ref[2 * t], in_ref[2 * t + 1])
        out_ref[0 : PB // 2, t * 128 : (t + 1) * 128] = top
        out_ref[PB // 2 : PB, t * 128 : (t + 1) * 128] = bottom


def inverse_kernel(occ_ref, slot_ref, vir_ref, inv_ref, col_ref, v_ref):
    column = (lax.axis_index("x") * ZH + lax.axis_index("zh")) * K + lax.axis_index("k")
    group = lax.axis_index("y") * ZL + lax.axis_index("zl")
    first_row = vir_ref[pl.ds(column // 4, 1), :]
    v_ref[...] = jnp.broadcast_to(first_row, (128, 128)).T
    col_ref[...] = v_ref[pl.ds(pl.multiple_of((column % 4) * WA, WA), WA), :]
    second_row = vir_ref[pl.ds(group // 2, 1), :]
    low1 = lax.broadcasted_iota(jnp.int32, (1, 128), 1) < 64
    swapped_row = pltpu.roll(jnp.broadcast_to(second_row, (8, 128)), 64, 1)[:1]
    odd = group % 2 == 1
    v_second = jnp.where(low1 != odd, second_row, swapped_row)

    @pl.loop(0, NOCC // 2)
    def _(big_j):
        lanes = pl.ds(pl.multiple_of(big_j * 128, 128), 128)
        occ_even = occ_ref[slot_ref[2 * big_j]]
        occ_odd = occ_ref[slot_ref[2 * big_j + 1]]
        second = jnp.where(low1, occ_even, occ_odd) - v_second - col_ref[...]
        for i in range(NOCC):
            inv_ref[i * WA : (i + 1) * WA, lanes] = 1.0 / (second + occ_ref[slot_ref[i]])


def levels_kernel(occ_ref, slot_ref, vir_ref, out_ref, v_ref):
    column = (lax.axis_index("x") * ZH + lax.axis_index("zh")) * K + lax.axis_index("k")
    group = lax.axis_index("y") * ZL + lax.axis_index("zl")
    first_row = vir_ref[pl.ds(column // 4, 1), :]
    v_ref[...] = jnp.broadcast_to(first_row, (128, 128)).T
    first = v_ref[pl.ds(pl.multiple_of((column % 4) * WA, WA), WA), :]
    second_row = vir_ref[pl.ds(group // 2, 1), :]
    low1 = lax.broadcasted_iota(jnp.int32, (1, 128), 1) < 64
    swapped_row = pltpu.roll(jnp.broadcast_to(second_row, (8, 128)), 64, 1)[:1]
    odd = group % 2 == 1
    v_second = jnp.where(low1 != odd, second_row, swapped_row)
    for t in range(NOCC // 2):
        occ = jnp.where(low1, occ_ref[slot_ref[2 * t]], occ_ref[slot_ref[2 * t + 1]])
        out_ref[:WA, t * 128 : (t + 1) * 128] = occ - v_second - first
    for i in range(NOCC):
        out_ref[WA + i : WA + i + 1, :128] = jnp.broadcast_to(occ_ref[slot_ref[i]], (1, 128))


def main_kernel(l_ref, levels_ref, *refs):
    blocks, (amp_ref, energy_ref, x_ref, z_ref) = refs[:-4], refs[-4:]
    starts = [sum(ref.shape[0] for ref in blocks[:n]) for n in range(len(blocks))]
    groups = AUX // GROUP
    low = low_half(WA)
    z_ref[...] = jnp.zeros_like(z_ref)

    def at(i, tile):
        return slice(i * WA, (i + 1) * WA), slice(tile * 128, (tile + 1) * 128)

    def product(n, g=groups - 1):
        lanes = slice(n * STEP, (n + 1) * STEP)
        parts = []
        for start, ref in zip(starts, blocks):
            if start // GROUP == g:
                inner = slice(start, start + ref.shape[0])
                parts.append(jnp.dot(l_ref[:, inner], ref[:, lanes], preferred_element_type=jnp.float32))
        total = sum(parts[1:], parts[0])
        x_ref[:, lanes] = total if g == 0 else x_ref[:, lanes] + total

    def ratios(big_i, big_j):
        if big_i <= big_j:
            s0 = x_ref[at(2 * big_j, big_i)]
            s1 = x_ref[at(2 * big_j + 1, big_i)]
            swaps = (jnp.where(low, s0, pltpu.roll(s1, 64, 1)), jnp.where(low, pltpu.roll(s0, 64, 1), s1))
        for e in range(2):
            i = 2 * big_i + e
            value = x_ref[at(i, big_j)]
            ratio = value / (levels_ref[:WA, big_j * 128 : (big_j + 1) * 128] + levels_ref[WA + i : WA + i + 1, :128])
            amp_ref[at(i, big_j)] = ratio.astype(jnp.bfloat16)
            if big_i <= big_j:
                part = ratio * (2.0 * value - swaps[e])
                z_ref[i * 8 : (i + 1) * 8, big_j * 128 : (big_j + 1) * 128] = jnp.sum(part.reshape(WA // 8, 8, 128), axis=0)

    def finish(n):
        width = STEP // 128
        for new in range(n * width, (n + 1) * width):
            for old in range(new + 1):
                ratios(old, new)
                if old < new:
                    ratios(new, old)

    for g in range(groups):
        for n in range(COLS // STEP if g < groups - 1 else 1):
            product(n, g)
    for n in range(1, COLS // STEP):
        product(n)
        finish(n - 1)
    finish(COLS // STEP - 1)

    source = lax.broadcasted_iota(jnp.int32, (COLS, 128), 0) // WB
    target = lax.broadcasted_iota(jnp.int32, (COLS, 128), 1) % NOCC
    chooser = jnp.where(source == target, 1.0, 0.0)
    by_pair = jnp.dot(z_ref[...], chooser, preferred_element_type=jnp.float32, precision=lax.Precision.HIGHEST)
    row = (lax.broadcasted_iota(jnp.int32, (NOCC * 8, 128), 0) // 8) % 8
    lane = lax.broadcasted_iota(jnp.int32, (NOCC * 8, 128), 1) // NOCC
    kept = jnp.where(row == lane, by_pair, 0.0)
    halves = [jnp.sum(kept[h * 64 : (h + 1) * 64], axis=0, keepdims=True) for h in range(2)]
    energy = jnp.concatenate(halves, axis=0)
    for z in range(ZL * ZH * K):
        energy_ref[z] = energy


def middle_kernel(in_ref, out_ref):
    total = jnp.sum(in_ref[...], axis=0)
    for n in range(Y * X):
        out_ref[n] = total


def last_kernel(in_ref, out_ref):
    total = jnp.sum(in_ref[...], axis=0) * (1.0 / (NV * NV))
    rows = jnp.concatenate([jnp.broadcast_to(total[h : h + 1], (8, 128)) for h in range(2)], axis=0)
    row = lax.broadcasted_iota(jnp.int32, (NOCC, 128), 0) % 8
    lane = lax.broadcasted_iota(jnp.int32, (NOCC, 128), 1) // NOCC
    kept = jnp.where(row == lane, rows, 0.0)
    source = lax.broadcasted_iota(jnp.int32, (128, NOCC), 0) % NOCC
    target = lax.broadcasted_iota(jnp.int32, (128, NOCC), 1)
    chooser = jnp.where(source == target, 1.0, 0.0)
    exact = dict(preferred_element_type=jnp.float32, precision=lax.Precision.HIGHEST)
    upper = jnp.dot(kept, chooser, **exact)
    mirror = lax.dot_general(chooser, kept, (((0,), (1,)), ((), ())), **exact)
    i = lax.broadcasted_iota(jnp.int32, (NOCC, NOCC), 0)
    j = lax.broadcasted_iota(jnp.int32, (NOCC, NOCC), 1)
    out_ref[...] = jnp.where(i <= j, upper, mirror)


def order_kernel(t_hbm, amp_ref, buf_ref, t_ref, sems):
    load = pltpu.make_async_copy(t_hbm, t_ref, sems.at[COLS // STEP])
    load.start()
    row = lax.broadcasted_iota(jnp.int32, (COLS, STEP), 0)
    lane = lax.broadcasted_iota(jnp.int32, (COLS, STEP), 1)
    copies = []
    for n in range(COLS // STEP):
        lanes = slice(n * STEP, (n + 1) * STEP)
        source = (lane % NOCC) * WB + lane // NOCC + n * (STEP // NOCC)
        chooser = jnp.where(row == source, 1.0, 0.0).astype(jnp.bfloat16)
        if n == 0:
            load.wait()
        buf_ref[:, lanes] = jnp.dot(t_ref[...], chooser, preferred_element_type=jnp.float32).astype(jnp.bfloat16)
        copies.append(pltpu.make_async_copy(buf_ref.at[:, lanes], amp_ref.at[:, lanes], sems.at[n]))
        copies[-1].start()
    for copy in copies:
        copy.wait()


def shape(dims, dtype=jnp.bfloat16):
    return jax.ShapeDtypeStruct(dims, dtype)


def call(kernel, out_shape, operands, in_specs=None, scratch=(), flops=0, out=VMEM, limit=16):
    kinds = in_specs or [VMEM] * len(operands)
    cost = pl.CostEstimate(flops=flops, bytes_accessed=4 * ROWS * COLS, transcendentals=0) if flops else None
    return pl.pallas_call(
        kernel,
        out_shape=out_shape,
        in_specs=kinds,
        out_specs=jax.tree.map(lambda _: out, out_shape),
        scratch_shapes=scratch,
        compiler_params=pltpu.CompilerParams(vmem_limit_bytes=limit * 1024 * 1024),
        cost_estimate=cost,
    )(*operands)


def run_main(left, levels, blocks):
    f32 = jnp.float32
    return call(
        main_kernel,
        (shape((ROWS, COLS)), shape((ZL * ZH * K, 2, 128), f32)),
        [left, levels] + blocks,
        scratch=[pltpu.VMEM((ROWS, COLS), f32), pltpu.VMEM((NOCC * 8, COLS), f32)],
    )


def run_order(ratio):
    return call(
        order_kernel,
        shape((ROWS, COLS)),
        [ratio],
        scratch=[pltpu.VMEM((ROWS, COLS), jnp.bfloat16), pltpu.VMEM((ROWS, COLS), jnp.bfloat16), pltpu.SemaphoreType.DMA((COLS // STEP + 1,))],
        in_specs=[ANY],
        limit=62,
        flops=2 * ROWS * COLS * COLS,
        out=ANY,
    )


def per_device(factors, occ_levels, vir_levels, slot_orbital):
    f32 = jnp.float32
    a1, a2 = call(
        prep_kernel,
        (shape((COL, WA // 2, 128)), shape((GRP, PB // 2, 128))),
        [factors.reshape(PB, NV)],
    )
    b1 = lax.all_to_all(a1, ("x", "zh", "k"), 0, 0, tiled=True)
    first = call(first_kernel, shape((Y, WA, AUX)), [b1])
    a2, _ = lax.optimization_barrier((a2, first))
    b2 = lax.all_to_all(a2, ("y", "zl"), 0, 0, tiled=True)
    first, b2 = lax.optimization_barrier((first, b2))
    own = lax.all_to_all(first, "y", 0, 0, tiled=True)
    second = call(second_kernel, shape((PB, COLS)), [b2])
    second = lax.all_gather(second, "zh", axis=0, tiled=True)
    near = lax.ppermute(own, "zl", [(0, 1), (1, 0)])
    up, down = [(i, (i + 1) % X) for i in range(X)], [(i, (i - 1) % X) for i in range(X)]
    below, above = lax.ppermute(second, "x", up), lax.ppermute(second, "x", down)
    second, own = lax.optimization_barrier((second, own))
    far = [lax.ppermute(below[: CHUNK // 2], "x", up), lax.ppermute(above[CHUNK // 2 :], "x", down)]
    mine = [second, below, above, jnp.concatenate(far, axis=0)]
    other = [lax.ppermute(block, "k", [(0, 1), (1, 0)]) for block in mine]
    blocks = [side[n] for n in range(4) for side in (mine, other)]
    left = call(place_kernel, shape((Y, ZL, WA, AUX)), [own, near]).reshape(ROWS, AUX)
    levels = call(
        levels_kernel,
        shape((WA + NOCC, COLS), f32),
        [occ_levels, slot_orbital, vir_levels.reshape(8, 128)],
        in_specs=[SMEM, SMEM, VMEM],
        scratch=[pltpu.VMEM((128, 128), f32)],
    )
    ratio, energy = run_main(left, levels, blocks)
    amp = run_order(ratio)
    energy = lax.all_to_all(energy, ("zl", "zh", "k"), 0, 0, tiled=True)
    energy = call(middle_kernel, shape((Y * X, 2, 128), f32), [energy])
    energy = lax.all_to_all(energy, ("y", "x"), 0, 0, tiled=True)
    return amp.reshape(NOCC, WA, COLS), call(last_kernel, shape((NOCC, NOCC), f32), [energy])


def solution(mesh):
    fine = Mesh(mesh.devices.reshape(Y, ZL, X, ZH, K), ("y", "zl", "x", "zh", "k"))
    grp, col = ("y", "zl"), ("x", "zh", "k")
    return jax.shard_map(
        per_device,
        mesh=fine,
        in_specs=(P(col, grp, None), P(), P(), P()),
        out_specs=(P(None, col, grp), P()),
        check_vma=False,
    )
```

```python
import jax
import jax.numpy as jnp
import numpy as np
from jax import lax
from jax.experimental import pallas as pl
from jax.experimental.pallas import tpu as pltpu
from jax.sharding import Mesh, PartitionSpec as P

Y, ZL, X, ZH, K = 8, 2, 4, 4, 2
GRP, COL = Y * ZL, X * ZH * K
AUX, NV, NOCC = 2048, 1024, 16
PB = AUX // COL
WA = NV // COL
WB = NV // GRP
ROWS, COLS = NOCC * WA, NOCC * WB
STEP = 256
CHUNK = ZH * PB
ARRIVAL = tuple((d, rel) for d in (0, 1, 3, 2) for rel in range(K))
GROUP = 2 * CHUNK
VMEM = pl.BlockSpec(memory_space=pltpu.VMEM)
SMEM = pl.BlockSpec(memory_space=pltpu.SMEM)
ANY = pl.BlockSpec(memory_space=pl.ANY)


def low_half(rows):
    return lax.broadcasted_iota(jnp.int32, (rows, 128), 1) < 64


def turn(v):
    return pltpu.roll(v.astype(jnp.float32), 64, 1).astype(v.dtype)


def pair_halves(first, second):
    low = low_half(first.shape[0])
    return jnp.where(low, first, turn(second)), jnp.where(low, turn(first), second)


def prep_kernel(x_ref, a1_ref, a2_ref):
    low = low_half(WA // 2)
    for t in range(NV // 128):
        tile = x_ref[:, t * 128 : (t + 1) * 128]
        wide = tile.astype(jnp.float32)
        both = jnp.concatenate([wide, wide], axis=0).T
        for s in range(128 // WA):
            top = both[s * WA : s * WA + WA // 2]
            bottom = both[s * WA + WA // 2 : (s + 1) * WA]
            piece = jnp.where(low, top, bottom).astype(jnp.bfloat16)
            c = t * (128 // WA) + s
            a1_ref[c] = piece
        even, odd = pair_halves(tile[: PB // 2], tile[PB // 2 :])
        a2_ref[2 * t] = even
        a2_ref[2 * t + 1] = odd


def first_kernel(in_ref, out_ref, one_ref, sems):
    own_k, own_x = lax.axis_index("k"), lax.axis_index("x")
    for n, (d, rel) in enumerate(ARRIVAL):
        k = (own_k + rel) % K
        x = (own_x + X - d) % X
        for m in range(ZH // 2):
            base = (x * ZH + 2 * m) * K + k
            top, bottom = pair_halves(in_ref[base], in_ref[base + K])
            lanes = (n * ZH + 2 * m) * PB
            one_ref[0 : WA // 2, lanes : lanes + 128] = top
            one_ref[WA // 2 : WA, lanes : lanes + 128] = bottom
    copies = [pltpu.make_async_copy(one_ref, out_ref.at[y], sems.at[y]) for y in range(Y)]
    for copy in copies:
        copy.start()
    for copy in copies:
        copy.wait()


def place_kernel(own_ref, near_ref, out_ref):
    zl = lax.axis_index("zl")
    for y in range(Y):
        out_ref[y, zl] = own_ref[y]
        out_ref[y, 1 - zl] = near_ref[y]


def second_kernel(in_ref, out_ref):
    for t in range(NOCC // 2):
        top, bottom = pair_halves(in_ref[2 * t], in_ref[2 * t + 1])
        out_ref[0 : PB // 2, t * 128 : (t + 1) * 128] = top
        out_ref[PB // 2 : PB, t * 128 : (t + 1) * 128] = bottom


def inverse_kernel(occ_ref, slot_ref, vir_ref, inv_ref, col_ref, v_ref):
    column = (lax.axis_index("x") * ZH + lax.axis_index("zh")) * K + lax.axis_index("k")
    group = lax.axis_index("y") * ZL + lax.axis_index("zl")
    first_row = vir_ref[pl.ds(column // 4, 1), :]
    v_ref[...] = jnp.broadcast_to(first_row, (128, 128)).T
    col_ref[...] = v_ref[pl.ds(pl.multiple_of((column % 4) * WA, WA), WA), :]
    second_row = vir_ref[pl.ds(group // 2, 1), :]
    low1 = lax.broadcasted_iota(jnp.int32, (1, 128), 1) < 64
    swapped_row = pltpu.roll(jnp.broadcast_to(second_row, (8, 128)), 64, 1)[:1]
    odd = group % 2 == 1
    v_second = jnp.where(low1 != odd, second_row, swapped_row)

    @pl.loop(0, NOCC // 2)
    def _(big_j):
        lanes = pl.ds(pl.multiple_of(big_j * 128, 128), 128)
        occ_even = occ_ref[slot_ref[2 * big_j]]
        occ_odd = occ_ref[slot_ref[2 * big_j + 1]]
        second = jnp.where(low1, occ_even, occ_odd) - v_second - col_ref[...]
        for i in range(NOCC):
            inv_ref[i * WA : (i + 1) * WA, lanes] = 1.0 / (second + occ_ref[slot_ref[i]])


def levels_kernel(occ_ref, slot_ref, vir_ref, out_ref, v_ref):
    column = (lax.axis_index("x") * ZH + lax.axis_index("zh")) * K + lax.axis_index("k")
    group = lax.axis_index("y") * ZL + lax.axis_index("zl")
    first_row = vir_ref[pl.ds(column // 4, 1), :]
    v_ref[...] = jnp.broadcast_to(first_row, (128, 128)).T
    first = v_ref[pl.ds(pl.multiple_of((column % 4) * WA, WA), WA), :]
    second_row = vir_ref[pl.ds(group // 2, 1), :]
    low1 = lax.broadcasted_iota(jnp.int32, (1, 128), 1) < 64
    swapped_row = pltpu.roll(jnp.broadcast_to(second_row, (8, 128)), 64, 1)[:1]
    odd = group % 2 == 1
    v_second = jnp.where(low1 != odd, second_row, swapped_row)
    for t in range(NOCC // 2):
        occ = jnp.where(low1, occ_ref[slot_ref[2 * t]], occ_ref[slot_ref[2 * t + 1]])
        out_ref[:WA, t * 128 : (t + 1) * 128] = occ - v_second - first
    for i in range(NOCC):
        out_ref[WA + i : WA + i + 1, :128] = jnp.broadcast_to(occ_ref[slot_ref[i]], (1, 128))


def main_kernel(l_ref, levels_ref, *refs):
    blocks, (amp_ref, energy_ref, x_ref, z_ref) = refs[:-4], refs[-4:]
    starts = [sum(ref.shape[0] for ref in blocks[:n]) for n in range(len(blocks))]
    groups = AUX // GROUP
    low = low_half(WA)
    z_ref[...] = jnp.zeros_like(z_ref)

    def at(i, tile):
        return slice(i * WA, (i + 1) * WA), slice(tile * 128, (tile + 1) * 128)

    def product(n, g=groups - 1):
        lanes = slice(n * STEP, (n + 1) * STEP)
        parts = []
        for start, ref in zip(starts, blocks):
            if start // GROUP == g:
                inner = slice(start, start + ref.shape[0])
                parts.append(jnp.dot(l_ref[:, inner], ref[:, lanes], preferred_element_type=jnp.float32))
        total = sum(parts[1:], parts[0])
        x_ref[:, lanes] = total if g == 0 else x_ref[:, lanes] + total

    def ratios(big_i, big_j):
        if big_i <= big_j:
            s0 = x_ref[at(2 * big_j, big_i)]
            s1 = x_ref[at(2 * big_j + 1, big_i)]
            swaps = (jnp.where(low, s0, pltpu.roll(s1, 64, 1)), jnp.where(low, pltpu.roll(s0, 64, 1), s1))
        for e in range(2):
            i = 2 * big_i + e
            value = x_ref[at(i, big_j)]
            ratio = value / (levels_ref[:WA, big_j * 128 : (big_j + 1) * 128] + levels_ref[WA + i : WA + i + 1, :128])
            amp_ref[at(i, big_j)] = ratio.astype(jnp.bfloat16)
            if big_i <= big_j:
                part = ratio * (2.0 * value - swaps[e])
                z_ref[i * 8 : (i + 1) * 8, big_j * 128 : (big_j + 1) * 128] = jnp.sum(part.reshape(WA // 8, 8, 128), axis=0)

    def finish(n):
        width = STEP // 128
        for new in range(n * width, (n + 1) * width):
            for old in range(new + 1):
                ratios(old, new)
                if old < new:
                    ratios(new, old)

    for g in range(groups):
        for n in range(COLS // STEP if g < groups - 1 else 1):
            product(n, g)
    for n in range(1, COLS // STEP):
        product(n)
        finish(n - 1)
    finish(COLS // STEP - 1)

    source = lax.broadcasted_iota(jnp.int32, (COLS, 128), 0) // WB
    target = lax.broadcasted_iota(jnp.int32, (COLS, 128), 1) % NOCC
    chooser = jnp.where(source == target, 1.0, 0.0)
    by_pair = jnp.dot(z_ref[...], chooser, preferred_element_type=jnp.float32, precision=lax.Precision.HIGHEST)
    row = (lax.broadcasted_iota(jnp.int32, (NOCC * 8, 128), 0) // 8) % 8
    lane = lax.broadcasted_iota(jnp.int32, (NOCC * 8, 128), 1) // NOCC
    kept = jnp.where(row == lane, by_pair, 0.0)
    halves = [jnp.sum(kept[h * 64 : (h + 1) * 64], axis=0, keepdims=True) for h in range(2)]
    energy = jnp.concatenate(halves, axis=0)
    for z in range(ZL * ZH * K):
        energy_ref[z] = energy


def middle_kernel(in_ref, out_ref):
    total = jnp.sum(in_ref[...], axis=0)
    for n in range(Y * X):
        out_ref[n] = total


def last_kernel(in_ref, out_ref):
    total = jnp.sum(in_ref[...], axis=0) * (1.0 / (NV * NV))
    rows = jnp.concatenate([jnp.broadcast_to(total[h : h + 1], (8, 128)) for h in range(2)], axis=0)
    row = lax.broadcasted_iota(jnp.int32, (NOCC, 128), 0) % 8
    lane = lax.broadcasted_iota(jnp.int32, (NOCC, 128), 1) // NOCC
    kept = jnp.where(row == lane, rows, 0.0)
    source = lax.broadcasted_iota(jnp.int32, (128, NOCC), 0) % NOCC
    target = lax.broadcasted_iota(jnp.int32, (128, NOCC), 1)
    chooser = jnp.where(source == target, 1.0, 0.0)
    exact = dict(preferred_element_type=jnp.float32, precision=lax.Precision.HIGHEST)
    upper = jnp.dot(kept, chooser, **exact)
    mirror = lax.dot_general(chooser, kept, (((0,), (1,)), ((), ())), **exact)
    i = lax.broadcasted_iota(jnp.int32, (NOCC, NOCC), 0)
    j = lax.broadcasted_iota(jnp.int32, (NOCC, NOCC), 1)
    out_ref[...] = jnp.where(i <= j, upper, mirror)


def order_kernel(t_hbm, amp_ref, buf_ref, t_ref, sems):
    load = pltpu.make_async_copy(t_hbm, t_ref, sems.at[COLS // STEP])
    load.start()
    row = lax.broadcasted_iota(jnp.int32, (COLS, STEP), 0)
    lane = lax.broadcasted_iota(jnp.int32, (COLS, STEP), 1)
    copies = []
    for n in range(COLS // STEP):
        lanes = slice(n * STEP, (n + 1) * STEP)
        source = (lane % NOCC) * WB + lane // NOCC + n * (STEP // NOCC)
        chooser = jnp.where(row == source, 1.0, 0.0).astype(jnp.bfloat16)
        if n == 0:
            load.wait()
        buf_ref[:, lanes] = jnp.dot(t_ref[...], chooser, preferred_element_type=jnp.float32).astype(jnp.bfloat16)
        copies.append(pltpu.make_async_copy(buf_ref.at[:, lanes], amp_ref.at[:, lanes], sems.at[n]))
        copies[-1].start()
    for copy in copies:
        copy.wait()


def shape(dims, dtype=jnp.bfloat16):
    return jax.ShapeDtypeStruct(dims, dtype)


def call(kernel, out_shape, operands, in_specs=None, scratch=(), flops=0, out=VMEM, limit=16):
    kinds = in_specs or [VMEM] * len(operands)
    cost = pl.CostEstimate(flops=flops, bytes_accessed=4 * ROWS * COLS, transcendentals=0) if flops else None
    return pl.pallas_call(
        kernel,
        out_shape=out_shape,
        in_specs=kinds,
        out_specs=jax.tree.map(lambda _: out, out_shape),
        scratch_shapes=scratch,
        compiler_params=pltpu.CompilerParams(vmem_limit_bytes=limit * 1024 * 1024),
        cost_estimate=cost,
    )(*operands)


def run_main(left, levels, blocks):
    f32 = jnp.float32
    return call(
        main_kernel,
        (shape((ROWS, COLS)), shape((ZL * ZH * K, 2, 128), f32)),
        [left, levels] + blocks,
        scratch=[pltpu.VMEM((ROWS, COLS), f32), pltpu.VMEM((NOCC * 8, COLS), f32)],
    )


def run_order(ratio):
    return call(
        order_kernel,
        shape((ROWS, COLS)),
        [ratio],
        scratch=[pltpu.VMEM((ROWS, COLS), jnp.bfloat16), pltpu.VMEM((ROWS, COLS), jnp.bfloat16), pltpu.SemaphoreType.DMA((COLS // STEP + 1,))],
        in_specs=[ANY],
        limit=62,
        flops=2 * ROWS * COLS * COLS,
        out=ANY,
    )


def per_device(factors, occ_levels, vir_levels, slot_orbital):
    f32 = jnp.float32
    a1, a2 = call(
        prep_kernel,
        (shape((COL, WA // 2, 128)), shape((GRP, PB // 2, 128))),
        [factors.reshape(PB, NV)],
    )
    b1 = lax.all_to_all(a1, ("x", "zh", "k"), 0, 0, tiled=True)
    first = call(
        first_kernel,
        shape((Y, WA, AUX)),
        [b1],
        scratch=[pltpu.VMEM((WA, AUX), jnp.bfloat16), pltpu.SemaphoreType.DMA((Y,))],
        out=ANY,
    )
    a2, _ = lax.optimization_barrier((a2, first))
    b2 = lax.all_to_all(a2, ("y", "zl"), 0, 0, tiled=True)
    first, b2 = lax.optimization_barrier((first, b2))
    own = lax.all_to_all(first, "y", 0, 0, tiled=True)
    second = call(second_kernel, shape((PB, COLS)), [b2])
    second = lax.all_gather(second, "zh", axis=0, tiled=True)
    near = lax.ppermute(own, "zl", [(0, 1), (1, 0)])
    up, down = [(i, (i + 1) % X) for i in range(X)], [(i, (i - 1) % X) for i in range(X)]
    below, above = lax.ppermute(second, "x", up), lax.ppermute(second, "x", down)
    second, own = lax.optimization_barrier((second, own))
    far = [lax.ppermute(below[: CHUNK // 2], "x", up), lax.ppermute(above[CHUNK // 2 :], "x", down)]
    mine = [second, below, above, jnp.concatenate(far, axis=0)]
    other = [lax.ppermute(block, "k", [(0, 1), (1, 0)]) for block in mine]
    blocks = [side[n] for n in range(4) for side in (mine, other)]
    left = call(place_kernel, shape((Y, ZL, WA, AUX)), [own, near]).reshape(ROWS, AUX)
    levels = call(
        levels_kernel,
        shape((WA + NOCC, COLS), f32),
        [occ_levels, slot_orbital, vir_levels.reshape(8, 128)],
        in_specs=[SMEM, SMEM, VMEM],
        scratch=[pltpu.VMEM((128, 128), f32)],
    )
    ratio, energy = run_main(left, levels, blocks)
    amp = run_order(ratio)
    energy = lax.all_to_all(energy, ("zl", "zh", "k"), 0, 0, tiled=True)
    energy, amp = lax.optimization_barrier((energy, amp))
    energy = call(middle_kernel, shape((Y * X, 2, 128), f32), [energy])
    energy = lax.all_to_all(energy, ("y", "x"), 0, 0, tiled=True)
    return amp.reshape(NOCC, WA, COLS), call(last_kernel, shape((NOCC, NOCC), f32), [energy])


def solution(mesh):
    fine = Mesh(mesh.devices.reshape(Y, ZL, X, ZH, K), ("y", "zl", "x", "zh", "k"))
    grp, col = ("y", "zl"), ("x", "zh", "k")
    return jax.shard_map(
        per_device,
        mesh=fine,
        in_specs=(P(col, grp, None), P(), P(), P()),
        out_specs=(P(None, col, grp), P()),
        check_vma=False,
    )
```

```python
import jax
import jax.numpy as jnp
import numpy as np
from jax import lax
from jax.experimental import pallas as pl
from jax.experimental.pallas import tpu as pltpu
from jax.sharding import Mesh, PartitionSpec as P

Y, ZL, X, ZH, K = 8, 2, 4, 4, 2
GRP, COL = Y * ZL, X * ZH * K
AUX, NV, NOCC = 2048, 1024, 16
PB = AUX // COL
WA = NV // COL
WB = NV // GRP
ROWS, COLS = NOCC * WA, NOCC * WB
STEP = 256
CHUNK = ZH * PB
ARRIVAL = tuple((d, rel) for d in (0, 1, 3, 2) for rel in range(K))
GROUP = 2 * CHUNK
VMEM = pl.BlockSpec(memory_space=pltpu.VMEM)
SMEM = pl.BlockSpec(memory_space=pltpu.SMEM)
ANY = pl.BlockSpec(memory_space=pl.ANY)


def low_half(rows):
    return lax.broadcasted_iota(jnp.int32, (rows, 128), 1) < 64


def turn(v):
    return pltpu.roll(v.astype(jnp.float32), 64, 1).astype(v.dtype)


def pair_halves(first, second):
    low = low_half(first.shape[0])
    return jnp.where(low, first, turn(second)), jnp.where(low, turn(first), second)


def prep_kernel(x_ref, a1_ref, a2_ref):
    low = low_half(WA // 2)
    for t in range(NV // 128):
        tile = x_ref[:, t * 128 : (t + 1) * 128]
        wide = tile.astype(jnp.float32)
        both = jnp.concatenate([wide, wide], axis=0).T
        for s in range(128 // WA):
            top = both[s * WA : s * WA + WA // 2]
            bottom = both[s * WA + WA // 2 : (s + 1) * WA]
            piece = jnp.where(low, top, bottom).astype(jnp.bfloat16)
            c = t * (128 // WA) + s
            a1_ref[c] = piece
        even, odd = pair_halves(tile[: PB // 2], tile[PB // 2 :])
        a2_ref[2 * t] = even
        a2_ref[2 * t + 1] = odd


def first_kernel(in_ref, out_ref, one_ref, sems):
    own_k, own_x = lax.axis_index("k"), lax.axis_index("x")
    for n, (d, rel) in enumerate(ARRIVAL):
        k = (own_k + rel) % K
        x = (own_x + X - d) % X
        for m in range(ZH // 2):
            base = (x * ZH + 2 * m) * K + k
            top, bottom = pair_halves(in_ref[base], in_ref[base + K])
            lanes = (n * ZH + 2 * m) * PB
            one_ref[0 : WA // 2, lanes : lanes + 128] = top
            one_ref[WA // 2 : WA, lanes : lanes + 128] = bottom
    copies = [pltpu.make_async_copy(one_ref, out_ref.at[y], sems.at[y]) for y in range(Y)]
    for copy in copies:
        copy.start()
    for copy in copies:
        copy.wait()


def own_kernel(own_ref, out_ref):
    zl = lax.axis_index("zl")
    for y in range(Y):
        out_ref[y, zl] = own_ref[y]


def near_kernel(held_ref, near_ref, out_ref):
    zl = lax.axis_index("zl")
    for y in range(Y):
        out_ref[y, 1 - zl] = near_ref[y]


def second_kernel(in_ref, out_ref):
    for t in range(NOCC // 2):
        top, bottom = pair_halves(in_ref[2 * t], in_ref[2 * t + 1])
        out_ref[0 : PB // 2, t * 128 : (t + 1) * 128] = top
        out_ref[PB // 2 : PB, t * 128 : (t + 1) * 128] = bottom


def inverse_kernel(occ_ref, slot_ref, vir_ref, inv_ref, col_ref, v_ref):
    column = (lax.axis_index("x") * ZH + lax.axis_index("zh")) * K + lax.axis_index("k")
    group = lax.axis_index("y") * ZL + lax.axis_index("zl")
    first_row = vir_ref[pl.ds(column // 4, 1), :]
    v_ref[...] = jnp.broadcast_to(first_row, (128, 128)).T
    col_ref[...] = v_ref[pl.ds(pl.multiple_of((column % 4) * WA, WA), WA), :]
    second_row = vir_ref[pl.ds(group // 2, 1), :]
    low1 = lax.broadcasted_iota(jnp.int32, (1, 128), 1) < 64
    swapped_row = pltpu.roll(jnp.broadcast_to(second_row, (8, 128)), 64, 1)[:1]
    odd = group % 2 == 1
    v_second = jnp.where(low1 != odd, second_row, swapped_row)

    @pl.loop(0, NOCC // 2)
    def _(big_j):
        lanes = pl.ds(pl.multiple_of(big_j * 128, 128), 128)
        occ_even = occ_ref[slot_ref[2 * big_j]]
        occ_odd = occ_ref[slot_ref[2 * big_j + 1]]
        second = jnp.where(low1, occ_even, occ_odd) - v_second - col_ref[...]
        for i in range(NOCC):
            inv_ref[i * WA : (i + 1) * WA, lanes] = 1.0 / (second + occ_ref[slot_ref[i]])


def levels_kernel(occ_ref, slot_ref, vir_ref, out_ref, v_ref):
    column = (lax.axis_index("x") * ZH + lax.axis_index("zh")) * K + lax.axis_index("k")
    group = lax.axis_index("y") * ZL + lax.axis_index("zl")
    first_row = vir_ref[pl.ds(column // 4, 1), :]
    v_ref[...] = jnp.broadcast_to(first_row, (128, 128)).T
    first = v_ref[pl.ds(pl.multiple_of((column % 4) * WA, WA), WA), :]
    second_row = vir_ref[pl.ds(group // 2, 1), :]
    low1 = lax.broadcasted_iota(jnp.int32, (1, 128), 1) < 64
    swapped_row = pltpu.roll(jnp.broadcast_to(second_row, (8, 128)), 64, 1)[:1]
    odd = group % 2 == 1
    v_second = jnp.where(low1 != odd, second_row, swapped_row)
    for t in range(NOCC // 2):
        occ = jnp.where(low1, occ_ref[slot_ref[2 * t]], occ_ref[slot_ref[2 * t + 1]])
        out_ref[:WA, t * 128 : (t + 1) * 128] = occ - v_second - first
    for i in range(NOCC):
        out_ref[WA + i : WA + i + 1, :128] = jnp.broadcast_to(occ_ref[slot_ref[i]], (1, 128))


def main_kernel(l_ref, levels_ref, *refs):
    blocks, (amp_ref, energy_ref, x_ref, z_ref) = refs[:-4], refs[-4:]
    starts = [sum(ref.shape[0] for ref in blocks[:n]) for n in range(len(blocks))]
    groups = AUX // GROUP
    low = low_half(WA)
    z_ref[...] = jnp.zeros_like(z_ref)

    def at(i, tile):
        return slice(i * WA, (i + 1) * WA), slice(tile * 128, (tile + 1) * 128)

    def product(n, g=groups - 1):
        lanes = slice(n * STEP, (n + 1) * STEP)
        parts = []
        for start, ref in zip(starts, blocks):
            if start // GROUP == g:
                inner = slice(start, start + ref.shape[0])
                parts.append(jnp.dot(l_ref[:, inner], ref[:, lanes], preferred_element_type=jnp.float32))
        total = sum(parts[1:], parts[0])
        x_ref[:, lanes] = total if g == 0 else x_ref[:, lanes] + total

    def ratios(big_i, big_j):
        if big_i <= big_j:
            s0 = x_ref[at(2 * big_j, big_i)]
            s1 = x_ref[at(2 * big_j + 1, big_i)]
            swaps = (jnp.where(low, s0, pltpu.roll(s1, 64, 1)), jnp.where(low, pltpu.roll(s0, 64, 1), s1))
        for e in range(2):
            i = 2 * big_i + e
            value = x_ref[at(i, big_j)]
            ratio = value / (levels_ref[:WA, big_j * 128 : (big_j + 1) * 128] + levels_ref[WA + i : WA + i + 1, :128])
            amp_ref[at(i, big_j)] = ratio.astype(jnp.bfloat16)
            if big_i <= big_j:
                part = ratio * (2.0 * value - swaps[e])
                z_ref[i * 8 : (i + 1) * 8, big_j * 128 : (big_j + 1) * 128] = jnp.sum(part.reshape(WA // 8, 8, 128), axis=0)

    def finish(n):
        width = STEP // 128
        for new in range(n * width, (n + 1) * width):
            for old in range(new + 1):
                ratios(old, new)
                if old < new:
                    ratios(new, old)

    for g in range(groups):
        for n in range(COLS // STEP if g < groups - 1 else 1):
            product(n, g)
    for n in range(1, COLS // STEP):
        product(n)
        finish(n - 1)
    finish(COLS // STEP - 1)

    source = lax.broadcasted_iota(jnp.int32, (COLS, 128), 0) // WB
    target = lax.broadcasted_iota(jnp.int32, (COLS, 128), 1) % NOCC
    chooser = jnp.where(source == target, 1.0, 0.0)
    by_pair = jnp.dot(z_ref[...], chooser, preferred_element_type=jnp.float32, precision=lax.Precision.HIGHEST)
    row = (lax.broadcasted_iota(jnp.int32, (NOCC * 8, 128), 0) // 8) % 8
    lane = lax.broadcasted_iota(jnp.int32, (NOCC * 8, 128), 1) // NOCC
    kept = jnp.where(row == lane, by_pair, 0.0)
    halves = [jnp.sum(kept[h * 64 : (h + 1) * 64], axis=0, keepdims=True) for h in range(2)]
    energy = jnp.concatenate(halves, axis=0)
    for z in range(ZL * ZH * K):
        energy_ref[z] = energy


def middle_kernel(in_ref, out_ref):
    total = jnp.sum(in_ref[...], axis=0)
    for n in range(Y * X):
        out_ref[n] = total


def last_kernel(in_ref, out_ref):
    total = jnp.sum(in_ref[...], axis=0) * (1.0 / (NV * NV))
    rows = jnp.concatenate([jnp.broadcast_to(total[h : h + 1], (8, 128)) for h in range(2)], axis=0)
    row = lax.broadcasted_iota(jnp.int32, (NOCC, 128), 0) % 8
    lane = lax.broadcasted_iota(jnp.int32, (NOCC, 128), 1) // NOCC
    kept = jnp.where(row == lane, rows, 0.0)
    source = lax.broadcasted_iota(jnp.int32, (128, NOCC), 0) % NOCC
    target = lax.broadcasted_iota(jnp.int32, (128, NOCC), 1)
    chooser = jnp.where(source == target, 1.0, 0.0)
    exact = dict(preferred_element_type=jnp.float32, precision=lax.Precision.HIGHEST)
    upper = jnp.dot(kept, chooser, **exact)
    mirror = lax.dot_general(chooser, kept, (((0,), (1,)), ((), ())), **exact)
    i = lax.broadcasted_iota(jnp.int32, (NOCC, NOCC), 0)
    j = lax.broadcasted_iota(jnp.int32, (NOCC, NOCC), 1)
    out_ref[...] = jnp.where(i <= j, upper, mirror)


def order_kernel(t_hbm, amp_ref, buf_ref, t_ref, sems):
    load = pltpu.make_async_copy(t_hbm, t_ref, sems.at[COLS // STEP])
    load.start()
    row = lax.broadcasted_iota(jnp.int32, (COLS, STEP), 0)
    lane = lax.broadcasted_iota(jnp.int32, (COLS, STEP), 1)
    copies = []
    for n in range(COLS // STEP):
        lanes = slice(n * STEP, (n + 1) * STEP)
        source = (lane % NOCC) * WB + lane // NOCC + n * (STEP // NOCC)
        chooser = jnp.where(row == source, 1.0, 0.0).astype(jnp.bfloat16)
        if n == 0:
            load.wait()
        buf_ref[:, lanes] = jnp.dot(t_ref[...], chooser, preferred_element_type=jnp.float32).astype(jnp.bfloat16)
        copies.append(pltpu.make_async_copy(buf_ref.at[:, lanes], amp_ref.at[:, lanes], sems.at[n]))
        copies[-1].start()
    for copy in copies:
        copy.wait()


def shape(dims, dtype=jnp.bfloat16):
    return jax.ShapeDtypeStruct(dims, dtype)


def call(kernel, out_shape, operands, in_specs=None, scratch=(), flops=0, out=VMEM, limit=16, aliases=None):
    kinds = in_specs or [VMEM] * len(operands)
    cost = pl.CostEstimate(flops=flops, bytes_accessed=4 * ROWS * COLS, transcendentals=0) if flops else None
    return pl.pallas_call(
        kernel,
        out_shape=out_shape,
        in_specs=kinds,
        out_specs=jax.tree.map(lambda _: out, out_shape),
        scratch_shapes=scratch,
        input_output_aliases=aliases or {},
        compiler_params=pltpu.CompilerParams(vmem_limit_bytes=limit * 1024 * 1024),
        cost_estimate=cost,
    )(*operands)


def run_main(left, levels, blocks):
    f32 = jnp.float32
    return call(
        main_kernel,
        (shape((ROWS, COLS)), shape((ZL * ZH * K, 2, 128), f32)),
        [left, levels] + blocks,
        scratch=[pltpu.VMEM((ROWS, COLS), f32), pltpu.VMEM((NOCC * 8, COLS), f32)],
    )


def run_order(ratio):
    return call(
        order_kernel,
        shape((ROWS, COLS)),
        [ratio],
        scratch=[pltpu.VMEM((ROWS, COLS), jnp.bfloat16), pltpu.VMEM((ROWS, COLS), jnp.bfloat16), pltpu.SemaphoreType.DMA((COLS // STEP + 1,))],
        in_specs=[ANY],
        limit=62,
        flops=2 * ROWS * COLS * COLS,
        out=ANY,
    )


def per_device(factors, occ_levels, vir_levels, slot_orbital):
    f32 = jnp.float32
    a1, a2 = call(
        prep_kernel,
        (shape((COL, WA // 2, 128)), shape((GRP, PB // 2, 128))),
        [factors.reshape(PB, NV)],
    )
    b1 = lax.all_to_all(a1, ("x", "zh", "k"), 0, 0, tiled=True)
    first = call(
        first_kernel,
        shape((Y, WA, AUX)),
        [b1],
        scratch=[pltpu.VMEM((WA, AUX), jnp.bfloat16), pltpu.SemaphoreType.DMA((Y,))],
        out=ANY,
    )
    a2, _ = lax.optimization_barrier((a2, first))
    b2 = lax.all_to_all(a2, ("y", "zl"), 0, 0, tiled=True)
    first, b2 = lax.optimization_barrier((first, b2))
    own = lax.all_to_all(first, "y", 0, 0, tiled=True)
    second = call(second_kernel, shape((PB, COLS)), [b2])
    second = lax.all_gather(second, "zh", axis=0, tiled=True)
    near = lax.ppermute(own, "zl", [(0, 1), (1, 0)])
    up, down = [(i, (i + 1) % X) for i in range(X)], [(i, (i - 1) % X) for i in range(X)]
    below, above = lax.ppermute(second, "x", up), lax.ppermute(second, "x", down)
    second, own = lax.optimization_barrier((second, own))
    far = [lax.ppermute(below[: CHUNK // 2], "x", up), lax.ppermute(above[CHUNK // 2 :], "x", down)]
    mine = [second, below, above, jnp.concatenate(far, axis=0)]
    other = [lax.ppermute(block, "k", [(0, 1), (1, 0)]) for block in mine]
    blocks = [side[n] for n in range(4) for side in (mine, other)]
    held = call(own_kernel, shape((Y, ZL, WA, AUX)), [own])
    left = call(near_kernel, shape((Y, ZL, WA, AUX)), [held, near], aliases={0: 0}).reshape(ROWS, AUX)
    levels = call(
        levels_kernel,
        shape((WA + NOCC, COLS), f32),
        [occ_levels, slot_orbital, vir_levels.reshape(8, 128)],
        in_specs=[SMEM, SMEM, VMEM],
        scratch=[pltpu.VMEM((128, 128), f32)],
    )
    ratio, energy = run_main(left, levels, blocks)
    amp = run_order(ratio)
    energy = lax.all_to_all(energy, ("zl", "zh", "k"), 0, 0, tiled=True)
    energy, amp = lax.optimization_barrier((energy, amp))
    energy = call(middle_kernel, shape((Y * X, 2, 128), f32), [energy])
    energy = lax.all_to_all(energy, ("y", "x"), 0, 0, tiled=True)
    return amp.reshape(NOCC, WA, COLS), call(last_kernel, shape((NOCC, NOCC), f32), [energy])


def solution(mesh):
    fine = Mesh(mesh.devices.reshape(Y, ZL, X, ZH, K), ("y", "zl", "x", "zh", "k"))
    grp, col = ("y", "zl"), ("x", "zh", "k")
    return jax.shard_map(
        per_device,
        mesh=fine,
        in_specs=(P(col, grp, None), P(), P(), P()),
        out_specs=(P(None, col, grp), P()),
        check_vma=False,
    )
```
